32 devices in a mesh: seq: 8 (over z, x), tp: 4 (over y, core).
Axes of the slice: x: 2, y: 2, z: 4, core: 2. Of those that a mesh axis runs over, the one named last changes fastest.
Arguments:
- tokens_in: bfloat16 [8, 4, 2560], P(None, None, 'tp'), may hold values from -32 to 32
- attn_gain: bfloat16 [2560], replicated, may hold values from 0.25 to 1.75
- mlp_gain: bfloat16 [2560], replicated, may hold values from 0.25 to 1.75
- proj_query: bfloat16 [2560, 2560], P(None, 'tp'), may hold values from -0.125 to 0.125
- proj_key: bfloat16 [2560, 640], P(None, 'tp'), may hold values from -0.125 to 0.125
- proj_value: bfloat16 [2560, 640], P(None, 'tp'), may hold values from -0.125 to 0.125
- proj_out: bfloat16 [2560, 2560], P('tp'), may hold values from -0.125 to 0.125
- proj_gate: bfloat16 [2560, 3456], P(None, 'tp'), may hold values from -0.125 to 0.125
- proj_up: bfloat16 [2560, 3456], P(None, 'tp'), may hold values from -0.125 to 0.125
- proj_down: bfloat16 [3456, 2560], P('tp'), may hold values from -0.109375 to 0.109375
- long_keys: bfloat16 [4096, 8, 80], P('seq', 'tp'), may hold values from -340 to 340
- long_values: bfloat16 [4096, 8, 80], P('seq', 'tp'), may hold values from -6 to 6
- short_keys: bfloat16 [512, 8, 240], P('seq', 'tp'), may hold values from -340 to 340
- short_values: bfloat16 [512, 8, 240], P('seq', 'tp'), may hold values from -6 to 6
- long_seen: int32 [1], replicated, may hold values from 4096 to 8191
- short_len: int32 [3], replicated, may hold values from 1 to 504, as said below
Outputs:
- layer_out: bfloat16 [8, 4, 2560], P(None, None, 'tp')
The draws below stay inside these ranges and needn't reach their ends.
Inputs may be any that keep to these rules, and one draw needn't show every extreme that they name: `short_len`: some short request has exactly 504 cached tokens and some exactly 1.
All inputs are finite; a program needn't handle non-finite values.
Results may differ from the reference program's by a relative error of at most 0.01.
Values may be sent and summed in bfloat16 or wider, within the bound.
A program may use at most 128 MiB of HBM per device.

```python
import math
import jax
import jax.numpy as jnp
from jax import lax

D = 2560
HEADS = 32
KV_HEADS = 8
HD = 80
FF = 3456
WIN = 4096
SCAP = 512
STEPS = 8
LONG = 1
SHORT = 3


def draw_tokens_in(key, part):
    total_reqs = LONG + SHORT
    key_base, key_cols, key_rows = jax.random.split(jax.random.fold_in(key, 17), 3)
    col_ramp = 0.5 + jnp.arange(D, dtype=jnp.float32) / D
    col_scale = 10.0 ** (jax.random.uniform(key_cols, (D,), dtype=jnp.float32) - 0.5) * col_ramp
    base_draw = jax.random.truncated_normal(key_base, -4.0, 4.0, (STEPS, total_reqs, D), dtype=jnp.float32)
    row_scale = 10.0 ** (jax.random.uniform(key_rows, (STEPS, total_reqs, 1), dtype=jnp.float32) * 0.4 - 0.2)
    return (base_draw * col_scale * row_scale).astype(jnp.bfloat16)


def cache_key_draw(key, slots, requests):
    key_base = jax.random.fold_in(key, 0)
    base_draw = 2.0 * jax.random.truncated_normal(key_base, -3.0, 3.0, (slots, KV_HEADS, requests, HD), dtype=jnp.float32)
    return base_draw.reshape(slots, KV_HEADS, requests * HD).astype(jnp.bfloat16)


def draw_long_keys(key, part):
    return cache_key_draw(jax.random.fold_in(key, 23), WIN, LONG)


def draw_short_keys(key, part):
    return cache_key_draw(jax.random.fold_in(key, 29), SCAP, SHORT)


def draw_short_len(key, part):
    key_len, key_pick = jax.random.split(jax.random.fold_in(key, 41), 2)
    lengths = jax.random.randint(key_len, (SHORT,), 1, SCAP - STEPS + 1)
    pick_index = jax.random.randint(key_pick, (), 0, SHORT)
    slot_ids = jnp.arange(SHORT, dtype=jnp.int32)
    lengths = jnp.where(slot_ids == pick_index, SCAP - STEPS, lengths)
    lengths = jnp.where(slot_ids == (pick_index + 1) % SHORT, 1, lengths)
    return lengths.astype(jnp.int32)


def levels(key, dims, cuts, least, high):
    def one(dim, shards_of):
        draws = jax.random.uniform(jax.random.fold_in(jax.random.fold_in(key, 6), dim), (shards_of,), jnp.float32, least / len(cuts), high / len(cuts))
        return jnp.repeat(jnp.exp(draws), dims[dim] // shards_of).reshape((-1,) + (1,) * (len(dims) - dim - 1))

    factor_of = one(*cuts[0])
    for cut in cuts[1:]:
        factor_of = factor_of * one(*cut)
    return factor_of


def centred(stream_key, extent, scale, limit, pieces=(), kind=jnp.bfloat16):
    drawn = scale * jax.random.normal(stream_key, extent, jnp.float32)
    if pieces:
        drawn = drawn * levels(stream_key, extent, pieces, -0.22, 0.18)
    return jnp.clip(drawn, -limit, limit).astype(kind)


def setup_inputs(seed: int = 0) -> dict:
    arg_keys = jax.random.split(jax.random.key(seed), 17)
    return {
        "tokens_in": draw_tokens_in(jax.random.fold_in(arg_keys[16], 71), 0),
        "attn_gain": jnp.clip(1.0 + 0.15 * jax.random.normal(arg_keys[1], (D,), jnp.float32), 0.25, 1.75).astype(jnp.bfloat16),
        "mlp_gain": jnp.clip(1.0 + 0.15 * jax.random.normal(arg_keys[2], (D,), jnp.float32), 0.25, 1.75).astype(jnp.bfloat16),
        "proj_query": centred(arg_keys[3], (D, HEADS * HD), D ** -0.5, 0.125, ((1, 4),)),
        "proj_key": centred(arg_keys[4], (D, KV_HEADS * HD), D ** -0.5, 0.125, ((1, 4),)),
        "proj_value": centred(arg_keys[5], (D, KV_HEADS * HD), D ** -0.5, 0.125, ((1, 4),)),
        "proj_out": centred(arg_keys[6], (HEADS * HD, D), (HEADS * HD) ** -0.5, 0.125, ((0, 4),)),
        "proj_gate": centred(arg_keys[7], (D, FF), D ** -0.5, 0.125, ((1, 4),)),
        "proj_up": centred(arg_keys[8], (D, FF), D ** -0.5, 0.125, ((1, 4),)),
        "proj_down": centred(arg_keys[9], (FF, D), FF ** -0.5, 0.109375, ((0, 4),)),
        "long_keys": draw_long_keys(jax.random.fold_in(arg_keys[16], 71), 0),
        "long_values": centred(arg_keys[11], (WIN, KV_HEADS, LONG * HD), 2.0, 6.0, ((0, 8), (1, 4))),
        "short_keys": draw_short_keys(jax.random.fold_in(arg_keys[16], 71), 0),
        "short_values": centred(arg_keys[13], (SCAP, KV_HEADS, SHORT * HD), 2.0, 6.0, ((0, 8), (1, 4))),
        "long_seen": jax.random.randint(arg_keys[14], (LONG,), WIN, 2 * WIN).astype(jnp.int32),
        "short_len": draw_short_len(jax.random.fold_in(arg_keys[16], 71), 0),
    }


eps_norm = 1e-05
theta_base = 10000.0
masked_score = -1e+30

def rms_scaled(hidden_rows, norm_gain):
    mean_square = lax.optimization_barrier(jnp.mean(hidden_rows * hidden_rows, axis=-1, keepdims=True))
    return hidden_rows * lax.rsqrt(mean_square + eps_norm) * norm_gain.astype(jnp.float32)

def rotate(vectors, positions):
    half_width = vectors.shape[-1] // 2
    freq_index = jnp.arange(half_width, dtype=jnp.float32)
    frequency = theta_base ** (-2.0 * freq_index / vectors.shape[-1])
    angles = positions.astype(jnp.float32)[..., None] * frequency
    view_shape = angles.shape[:2] + (1,) * (vectors.ndim - 3) + (half_width,)
    cosine_table = jnp.cos(angles).reshape(view_shape)
    sine_table = jnp.sin(angles).reshape(view_shape)
    front_part = vectors[..., :half_width]
    back_part = vectors[..., half_width:]
    return jnp.concatenate([front_part * cosine_table - back_part * sine_table, back_part * cosine_table + front_part * sine_table], axis=-1)

def round_weights(weights):
    return lax.optimization_barrier(weights.astype(jnp.bfloat16)).astype(jnp.float32)

def attend(queries, cache_keys, cache_values, cache_valid, fresh_keys, fresh_values, fresh_valid):
    score_scale = 1.0 / math.sqrt(queries.shape[-1])
    query_float = queries.astype(jnp.float32)
    old_scores = jnp.einsum('trkgd,wkrd->trkgw', query_float, cache_keys.astype(jnp.float32)) * score_scale
    new_scores = jnp.einsum('trkgd,wkrd->trkgw', query_float, fresh_keys.astype(jnp.float32)) * score_scale
    old_mask = cache_valid[:, :, None, None, :]
    new_mask = fresh_valid[:, :, None, None, :]
    old_scores = jnp.where(old_mask, old_scores, masked_score)
    new_scores = jnp.where(new_mask, new_scores, masked_score)
    row_top = jnp.maximum(lax.optimization_barrier(jnp.max(old_scores, axis=-1)), lax.optimization_barrier(jnp.max(new_scores, axis=-1)))[..., None]
    old_weights = jnp.where(old_mask, jnp.exp(old_scores - row_top), 0.0)
    new_weights = jnp.where(new_mask, jnp.exp(new_scores - row_top), 0.0)
    weight_sum = lax.optimization_barrier(jnp.sum(old_weights, axis=-1)) + lax.optimization_barrier(jnp.sum(new_weights, axis=-1))
    weighted = jnp.einsum('trkgw,wkrd->trkgd', round_weights(old_weights), cache_values.astype(jnp.float32))
    weighted = weighted + jnp.einsum('trkgw,wkrd->trkgd', round_weights(new_weights), fresh_values.astype(jnp.float32))
    return weighted / weight_sum[..., None]

def reference(tokens_in, attn_gain, mlp_gain, proj_query, proj_key, proj_value, proj_out, proj_gate, proj_up, proj_down, long_keys, long_values, short_keys, short_values, long_seen, short_len):
    total_reqs = LONG + SHORT
    group_size = HEADS // KV_HEADS
    step_ids = jnp.arange(STEPS, dtype=jnp.int32)
    base_pos = jnp.concatenate([long_seen, short_len]).astype(jnp.int32)
    positions = step_ids[:, None] + base_pos[None, :]
    rows_in = tokens_in.astype(jnp.float32)
    normed = rms_scaled(rows_in, attn_gain).astype(jnp.bfloat16)
    flat_rows = normed.reshape(STEPS * total_reqs, D)
    queries = jnp.dot(flat_rows, proj_query, preferred_element_type=jnp.float32)
    queries = rotate(queries.reshape(STEPS, total_reqs, KV_HEADS, group_size, HD), positions).astype(jnp.bfloat16)
    new_keys = jnp.dot(flat_rows, proj_key, preferred_element_type=jnp.float32)
    new_keys = rotate(new_keys.reshape(STEPS, total_reqs, KV_HEADS, HD), positions).astype(jnp.bfloat16)
    new_keys = new_keys.transpose(0, 2, 1, 3)
    new_values = jnp.dot(flat_rows, proj_value, preferred_element_type=jnp.float32)
    new_values = new_values.reshape(STEPS, total_reqs, KV_HEADS, HD).astype(jnp.bfloat16).transpose(0, 2, 1, 3)
    fresh_valid = jnp.broadcast_to(step_ids[None, None, :] <= step_ids[:, None, None], (STEPS, total_reqs, STEPS))
    long_age = (jnp.arange(WIN, dtype=jnp.int32)[None, :] - (long_seen % WIN)[:, None]) % WIN
    long_valid = long_age[None, :, :] > step_ids[:, None, None]
    short_live = jnp.arange(SCAP, dtype=jnp.int32)[None, :] < short_len[:, None]
    short_valid = jnp.broadcast_to(short_live[None], (STEPS, SHORT, SCAP))
    long_out = attend(queries[:, :LONG], long_keys.reshape(WIN, KV_HEADS, LONG, HD), long_values.reshape(WIN, KV_HEADS, LONG, HD), long_valid, new_keys[:, :, :LONG], new_values[:, :, :LONG], fresh_valid[:, :LONG])
    short_out = attend(queries[:, LONG:], short_keys.reshape(SCAP, KV_HEADS, SHORT, HD), short_values.reshape(SCAP, KV_HEADS, SHORT, HD), short_valid, new_keys[:, :, LONG:], new_values[:, :, LONG:], fresh_valid[:, LONG:])
    attended = jnp.concatenate([long_out, short_out], axis=1).astype(jnp.bfloat16)
    attended = attended.reshape(STEPS * total_reqs, HEADS * HD)
    stream = rows_in + jnp.dot(attended, proj_out, preferred_element_type=jnp.float32).reshape(STEPS, total_reqs, D)
    mlp_in = rms_scaled(stream, mlp_gain).astype(jnp.bfloat16).reshape(STEPS * total_reqs, D)
    gate_act = jnp.dot(mlp_in, proj_gate, preferred_element_type=jnp.float32)
    up_act = jnp.dot(mlp_in, proj_up, preferred_element_type=jnp.float32)
    hidden_act = (jax.nn.silu(gate_act) * up_act).astype(jnp.bfloat16)
    down_act = jnp.dot(hidden_act, proj_down, preferred_element_type=jnp.float32).reshape(STEPS, total_reqs, D)
    return (stream + down_act).astype(jnp.bfloat16)
```

```python
import math

import jax
import jax.numpy as jnp
from jax import lax
from jax.sharding import PartitionSpec as P

HEADS = 32
KV_HEADS = 8
HD = 80
WIN = 4096
STEPS = 8
LONG = 1


eps_norm = 1e-05
theta_base = 10000.0
masked_score = -1e30


def rms_scaled(hidden_rows, norm_gain):
    mean_square = jnp.mean(hidden_rows * hidden_rows, axis=-1, keepdims=True)
    return hidden_rows * lax.rsqrt(mean_square + eps_norm) * norm_gain.astype(jnp.float32)


def rotate(vectors, positions):
    half_width = vectors.shape[-1] // 2
    freq_index = jnp.arange(half_width, dtype=jnp.float32)
    frequency = theta_base ** (-2.0 * freq_index / vectors.shape[-1])
    angles = positions.astype(jnp.float32)[..., None] * frequency
    view_shape = angles.shape[:2] + (1,) * (vectors.ndim - 3) + (half_width,)
    cosine_table = jnp.cos(angles).reshape(view_shape)
    sine_table = jnp.sin(angles).reshape(view_shape)
    front_part = vectors[..., :half_width]
    back_part = vectors[..., half_width:]
    return jnp.concatenate(
        [
            front_part * cosine_table - back_part * sine_table,
            back_part * cosine_table + front_part * sine_table,
        ],
        axis=-1,
    )


def partial_softmax(queries, cache_keys, cache_values, valid_mask):
    score_scale = 1.0 / math.sqrt(queries.shape[-1])
    scores = (
        jnp.einsum("trkgd,wkrd->trkgw", queries, cache_keys, preferred_element_type=jnp.float32)
        * score_scale
    )
    live_mask = valid_mask[:, :, None, None, :]
    scores = jnp.where(live_mask, scores, masked_score)
    top_score = jnp.max(scores, axis=-1)
    weights = jnp.where(live_mask, jnp.exp(scores - top_score[..., None]), 0.0)
    weight_sum = jnp.sum(weights, axis=-1)
    weighted = jnp.einsum(
        "trkgw,wkrd->trkgd",
        weights.astype(jnp.bfloat16),
        cache_values,
        preferred_element_type=jnp.float32,
    )
    return (top_score, weight_sum, weighted)


def body(
    tokens_in,
    attn_gain,
    mlp_gain,
    proj_query,
    proj_key,
    proj_value,
    proj_out,
    proj_gate,
    proj_up,
    proj_down,
    long_keys,
    long_values,
    short_keys,
    short_values,
    long_seen,
    short_len,
):
    seq_rank = lax.axis_index("seq")
    tp_rank = lax.axis_index("tp")
    local_width = tokens_in.shape[2]
    model_width = proj_query.shape[0]
    total_reqs = tokens_in.shape[1]
    group_size = HEADS // KV_HEADS
    kv_local = proj_key.shape[1] // HD
    base_pos = jnp.concatenate([long_seen, short_len])
    roll_start = long_seen % WIN
    long_slots = long_keys.shape[0]
    short_slots = short_keys.shape[0]
    long_global = seq_rank * long_slots + jnp.arange(long_slots, dtype=jnp.int32)
    long_age = (long_global[None, :] - roll_start[:, None]) % WIN
    short_global = seq_rank * short_slots + jnp.arange(short_slots, dtype=jnp.int32)
    short_live = short_global[None, :] < short_len[:, None]
    long_key_view = long_keys.reshape(long_slots, kv_local, LONG, HD)
    long_value_view = long_values.reshape(long_slots, kv_local, LONG, HD)
    short_key_view = short_keys.reshape(short_slots, kv_local, total_reqs - LONG, HD)
    short_value_view = short_values.reshape(short_slots, kv_local, total_reqs - LONG, HD)
    collected = []
    prior_keys = []
    prior_values = []
    for step_num in range(0, STEPS, STEPS):
        token_rows = tokens_in[step_num : step_num + STEPS]
        block_steps = token_rows.shape[0]
        full_rows = lax.all_gather(token_rows, "tp", axis=2, tiled=True)
        normed = rms_scaled(full_rows.astype(jnp.float32), attn_gain).astype(jnp.bfloat16)
        flat_rows = normed.reshape(block_steps * total_reqs, model_width)
        steps_here = step_num + jnp.arange(block_steps, dtype=jnp.int32)
        positions = steps_here[:, None] + base_pos[None, :]
        queries = jnp.dot(flat_rows, proj_query, preferred_element_type=jnp.float32)
        queries = rotate(
            queries.reshape(block_steps, total_reqs, kv_local, group_size, HD), positions
        ).astype(jnp.bfloat16)
        key_new = jnp.dot(flat_rows, proj_key, preferred_element_type=jnp.float32)
        key_new = rotate(key_new.reshape(block_steps, total_reqs, kv_local, HD), positions).astype(
            jnp.bfloat16
        )
        value_new = jnp.dot(flat_rows, proj_value, preferred_element_type=jnp.float32)
        value_new = value_new.reshape(block_steps, total_reqs, kv_local, HD).astype(jnp.bfloat16)
        every_key = jnp.concatenate(prior_keys + [key_new], axis=0).transpose(0, 2, 1, 3)
        every_value = jnp.concatenate(prior_values + [value_new], axis=0).transpose(0, 2, 1, 3)
        token_ids = jnp.arange(every_key.shape[0], dtype=jnp.int32)
        fresh_valid = jnp.broadcast_to(
            token_ids[None, None, :] <= steps_here[:, None, None],
            (block_steps, total_reqs, every_key.shape[0]),
        )
        long_valid = long_age[None, :, :] > steps_here[:, None, None]
        short_valid = short_live[None]
        long_part = partial_softmax(queries[:, :LONG], long_key_view, long_value_view, long_valid)
        short_part = partial_softmax(
            queries[:, LONG:], short_key_view, short_value_view, short_valid
        )
        old_top = jnp.concatenate([long_part[0], short_part[0]], axis=1)
        old_sum = jnp.concatenate([long_part[1], short_part[1]], axis=1)
        old_acc = jnp.concatenate([long_part[2], short_part[2]], axis=1)
        global_top = lax.pmax(old_top, "seq")
        rescale = jnp.exp(old_top - global_top)
        old_sum, old_acc = lax.psum((old_sum * rescale, old_acc * rescale[..., None]), "seq")
        old_top = global_top
        new_top, new_sum, new_acc = partial_softmax(queries, every_key, every_value, fresh_valid)
        both_top = jnp.maximum(old_top, new_top)
        old_factor = jnp.exp(old_top - both_top)
        new_factor = jnp.exp(new_top - both_top)
        attended = (old_acc * old_factor[..., None] + new_acc * new_factor[..., None]) / (
            old_sum * old_factor + new_sum * new_factor
        )[..., None]
        attended = attended.astype(jnp.bfloat16).reshape(
            block_steps * total_reqs, kv_local * group_size * HD
        )
        head_term = jnp.dot(attended, proj_out, preferred_element_type=jnp.float32).reshape(
            block_steps, total_reqs, model_width
        )
        stream_full = full_rows.astype(jnp.float32) + lax.psum(
            head_term.astype(jnp.bfloat16), "tp"
        ).astype(jnp.float32)
        mlp_in = rms_scaled(stream_full, mlp_gain).astype(jnp.bfloat16)
        stream = lax.dynamic_slice_in_dim(
            stream_full, tp_rank * local_width, local_width, stream_full.ndim - 1
        )
        mlp_flat = mlp_in.reshape(block_steps * total_reqs, model_width)
        gate_act = jnp.dot(mlp_flat, proj_gate, preferred_element_type=jnp.float32)
        up_act = jnp.dot(mlp_flat, proj_up, preferred_element_type=jnp.float32)
        hidden_act = (jax.nn.silu(gate_act) * up_act).astype(jnp.bfloat16)
        down_term = jnp.dot(hidden_act, proj_down, preferred_element_type=jnp.float32).reshape(
            block_steps, total_reqs, model_width
        )
        result = (
            stream
            + lax.psum_scatter(
                down_term.astype(jnp.bfloat16), "tp", scatter_dimension=2, tiled=True
            ).astype(jnp.float32)
        ).astype(jnp.bfloat16)
        result, key_new, value_new = (result, key_new, value_new)
        collected.append(result)
        prior_keys = prior_keys + [key_new]
        prior_values = prior_values + [value_new]
    output = jnp.concatenate(collected, axis=0)
    return output


def solution(mesh):
    in_specs = (
        P(None, None, "tp"),
        P(),
        P(),
        P(None, "tp"),
        P(None, "tp"),
        P(None, "tp"),
        P("tp", None),
        P(None, "tp"),
        P(None, "tp"),
        P("tp", None),
        P("seq", "tp", None),
        P("seq", "tp", None),
        P("seq", "tp", None),
        P("seq", "tp", None),
        P(),
        P(),
    )
    out_specs = P(None, None, "tp")
    return jax.shard_map(body, mesh=mesh, in_specs=in_specs, out_specs=out_specs, check_vma=False)
```

```python
import functools
import math

import jax
import jax.numpy as jnp
import numpy as np
from jax import lax
from jax.experimental import pallas as pl
from jax.experimental.pallas import tpu as pltpu
from jax.sharding import PartitionSpec as P

HEADS = 32
KV_HEADS = 8
HD = 80
HALF = HD // 2
GROUP = HEADS // KV_HEADS
WIN = 4096
STEPS = 8

EPS = 1e-05
THETA = 10000.0
HIDDEN_SCORE = -1e30
SCALE = 1.0 / math.sqrt(HD)
F32 = jnp.float32
BF16 = jnp.bfloat16
MESH = pl.DeviceIdType.MESH


def up_to(n, unit):
    return -(-n // unit) * unit


def dot(a, b):
    return lax.dot_general(a, b, (((1,), (0,)), ((), ())), preferred_element_type=F32)


def dot_t(a, b):
    return lax.dot_general(a, b, (((1,), (1,)), ((), ())), preferred_element_type=F32)


def pad_rows(v, rows):
    if v.shape[0] == rows:
        return v
    return jnp.concatenate([v, jnp.zeros((rows - v.shape[0], v.shape[1]), v.dtype)], axis=0)


def fold(v, rows):
    parts = []
    for low in range(0, v.shape[1], 128):
        part = v[:, low : min(low + 128, v.shape[1])]
        if part.shape[1] < 128:
            part = jnp.concatenate(
                [part, jnp.zeros((part.shape[0], 128 - part.shape[1]), v.dtype)], axis=1
            )
        parts.append(part)
    return pad_rows(jnp.concatenate(parts, axis=0), rows)


def unfold(v, n, width):
    parts = []
    for k, low in enumerate(range(0, width, 128)):
        parts.append(v[k * n : (k + 1) * n, : min(128, width - low)])
    return jnp.concatenate(parts, axis=1)


def sine_cosine(angle):
    turns = jnp.floor(angle * np.float32(2.0 / math.pi) + 0.5)
    rest = angle - turns * np.float32(1.5703125)
    rest = rest - turns * np.float32(4.8351287841796875e-4)
    rest = rest - turns * np.float32(math.pi / 2 - 1.5703125 - 4.8351287841796875e-4)
    sq = rest * rest
    sine = rest + rest * sq * (
        np.float32(-1.6666654611e-1)
        + sq * (np.float32(8.3321608736e-3) + sq * np.float32(-1.9515295891e-4))
    )
    cosine = 1.0 - 0.5 * sq + sq * sq * (
        np.float32(4.166664568298827e-2)
        + sq * (np.float32(-1.388731625493765e-3) + sq * np.float32(2.443315711809948e-5))
    )
    quarter = turns - 4.0 * jnp.floor(turns * 0.25)
    odd = (quarter == 1.0) | (quarter == 3.0)
    sin_out = jnp.where(odd, cosine, sine)
    cos_out = jnp.where(odd, sine, cosine)
    sin_out = jnp.where(quarter >= 2.0, -sin_out, sin_out)
    cos_out = jnp.where((quarter == 1.0) | (quarter == 2.0), -cos_out, cos_out)
    return sin_out, cos_out


def rope(v, cosine, signed_sine, front):
    ahead = jnp.concatenate([v[:, HALF:], v[:, :HALF]], axis=1)
    behind = jnp.concatenate([v[:, -HALF:], v[:, :-HALF]], axis=1)
    return v * cosine + jnp.where(front, ahead, behind) * signed_sine


def kernel(
    ns, nt, tok, ag, mg, wq, wk, wv, wo, wg, wu, wd, lk, lv, sk, sv, fr, seen, slen, out,
    tok_v, ag_v, mg_v, wq_v, wk_v, wv_v, wo_v, wg_v, wu_v, wd_v, lk_v, lv_v, sk_v, sv_v, fr_v,
    xg, sb, rb, ob, orb, stx, db, drb, frb, local_sem,
    x_send, x_recv, s_send, s_recv, o_send, o_recv, d_send, d_recv, f_send, f_recv,
):
    me_s = lax.axis_index("seq")
    me_t = lax.axis_index("tp")
    steps, reqs, dl = tok.shape
    rows = steps * reqs
    n_tok = rows // ns
    halves = steps // n_tok
    model = wq.shape[0]
    ql = wq.shape[1]
    kl = wk.shape[0]
    heads = ql // HD
    kvl = kl // HD
    long_slots = lk.shape[2]
    short_slots = sk.shape[0]
    fold_rows = frb.shape[1]

    pairs = [
        (tok, tok_v), (ag, ag_v), (fr, fr_v), (wq, wq_v), (wk, wk_v), (wv, wv_v),
        (lk, lk_v), (sk, sk_v), (lv, lv_v), (sv, sv_v), (wo, wo_v), (mg, mg_v),
        (wg, wg_v), (wu, wu_v), (wd, wd_v),
    ]
    copies = {}
    for i, (src, dst) in enumerate(pairs):
        copies[i] = pltpu.make_async_copy(src, dst, local_sem.at[i])
        copies[i].start()

    barrier = pltpu.get_barrier_semaphore()
    for d in range(1, nt):
        pl.semaphore_signal(
            barrier, inc=1, device_id=(me_s, lax.rem(me_t + d, nt)), device_id_type=MESH
        )
    for d in range(1, ns):
        pl.semaphore_signal(
            barrier, inc=1, device_id=(lax.rem(me_s + d, ns), me_t), device_id_type=MESH
        )

    copies[0].wait()
    by_step = [tok_v[t].astype(F32) for t in range(steps)]
    mine = jnp.concatenate(
        [by_step[t][r : r + 1] for r in range(reqs) for t in range(steps)], axis=0
    )
    xg[me_t] = mine.astype(BF16)
    pl.semaphore_wait(barrier, nt - 1 + ns - 1)

    def to_tp(src, dst, send, recv, d):
        return pltpu.make_async_remote_copy(
            src_ref=src, dst_ref=dst, send_sem=send.at[d - 1], recv_sem=recv.at[d - 1],
            device_id=(me_s, lax.rem(me_t + d, nt)), device_id_type=MESH,
        )

    def to_seq(src, dst, send, recv, d):
        return pltpu.make_async_remote_copy(
            src_ref=src, dst_ref=dst, send_sem=send.at[d - 1], recv_sem=recv.at[d - 1],
            device_id=(lax.rem(me_s + d, ns), me_t), device_id_type=MESH,
        )

    x_copies = [to_tp(xg.at[me_t], xg.at[me_t], x_send, x_recv, d) for d in range(1, nt)]
    for copy in x_copies:
        copy.start()

    copies[2].wait()
    row = lax.broadcasted_iota(jnp.int32, (rows, 1), 0)
    req = row // steps
    base = jnp.where(req == 0, seen[0], 0)
    for r in range(1, reqs):
        base = jnp.where(req == r, slen[r - 1], base)
    position = (base + row % steps).astype(F32)
    sine, cosine = sine_cosine(position * fr_v[...])
    lane = lax.broadcasted_iota(jnp.int32, (rows, ql), 1)
    front = lane % HD < HALF
    signed_sine = jnp.where(front, -sine, sine)

    for copy in x_copies:
        copy.wait()
    copies[1].wait()
    pieces = [xg[c].astype(F32) for c in range(nt)]
    square = jnp.zeros((rows, 1), F32)
    for piece in pieces:
        square = square + jnp.sum(piece * piece, axis=-1, keepdims=True)
    inverse = lax.rsqrt(square * np.float32(1.0 / model) + EPS)
    gain = ag_v[...].astype(F32)[None]
    normed = [
        (piece * inverse * gain[:, c * dl : (c + 1) * dl]).astype(BF16)
        for c, piece in enumerate(pieces)
    ]

    def project(parts, weight):
        total = None
        for c, part in enumerate(parts):
            term = dot(part, weight[c * dl : (c + 1) * dl, :])
            total = term if total is None else total + term
        return total

    def project_t(parts, weight):
        total = None
        for c, part in enumerate(parts):
            term = dot_t(part, weight[:, c * dl : (c + 1) * dl])
            total = term if total is None else total + term
        return total

    copies[3].wait()
    query = rope(project(normed, wq_v), cosine, signed_sine, front)
    copies[4].wait()
    key = rope(project_t(normed, wk_v), cosine[:, :kl], signed_sine[:, :kl], front[:, :kl])
    copies[5].wait()
    value = project_t(normed, wv_v)

    for i in (6, 7, 8, 9):
        copies[i].wait()
    short_k = sk_v[...].reshape(short_slots * kvl, sk.shape[2])
    short_v = sv_v[...].reshape(short_slots * kvl, sv.shape[2])
    row_count = heads * steps
    new_count = kvl * steps
    lane128 = lax.broadcasted_iota(jnp.int32, (row_count, 128), 1)
    for r in range(reqs):
        rs = slice(r * steps, (r + 1) * steps)
        q_r = jnp.concatenate(
            [query[rs, h * HD : (h + 1) * HD] for h in range(heads)], axis=0
        ).astype(BF16)
        k_r = jnp.concatenate(
            [key[rs, k * HD : (k + 1) * HD] for k in range(kvl)], axis=0
        ).astype(BF16)
        v_r = jnp.concatenate(
            [value[rs, k * HD : (k + 1) * HD] for k in range(kvl)], axis=0
        ).astype(BF16)
        step_of = lax.broadcasted_iota(jnp.int32, (row_count, 1), 0) % steps
        kv_of = lax.broadcasted_iota(jnp.int32, (row_count, 1), 0) // (steps * GROUP)
        if r == 0:
            col = lax.broadcasted_iota(jnp.int32, (1, long_slots), 1)
            slot = me_s * long_slots + col
            old_mask = ((slot - seen[0]) & (WIN - 1)) > step_of
            span = steps * GROUP
            old_dots = jnp.concatenate(
                [dot(q_r[k * span : (k + 1) * span], lk_v[k]) for k in range(kvl)], axis=0
            )
        else:
            cut = slice((r - 1) * HD, r * HD)
            col = lax.broadcasted_iota(jnp.int32, (1, short_slots * kvl), 1)
            slot = me_s * short_slots + col // kvl
            old_mask = (kv_of == col % kvl) & (slot < slen[r - 1])
            old_dots = dot_t(q_r, short_k[:, cut])
        new_col = lax.broadcasted_iota(jnp.int32, (1, new_count), 1)
        new_mask = (kv_of == new_col // steps) & (new_col % steps <= step_of) & (me_s == 0)
        old_score = jnp.where(old_mask, old_dots * SCALE, HIDDEN_SCORE)
        new_score = jnp.where(new_mask, dot_t(q_r, k_r) * SCALE, HIDDEN_SCORE)
        top = jnp.maximum(
            jnp.max(old_score, axis=-1, keepdims=True), jnp.max(new_score, axis=-1, keepdims=True)
        )
        old_w = jnp.where(old_mask, jnp.exp(old_score - top), 0.0)
        new_w = jnp.where(new_mask, jnp.exp(new_score - top), 0.0)
        total = jnp.sum(old_w, axis=-1, keepdims=True) + jnp.sum(new_w, axis=-1, keepdims=True)
        old_w = old_w.astype(BF16)
        if r == 0:
            acc = jnp.concatenate(
                [dot_t(old_w[k * span : (k + 1) * span], lv_v[k]) for k in range(kvl)], axis=0
            )
        else:
            acc = dot(old_w, short_v[:, cut])
        acc = acc + dot(new_w.astype(BF16), v_r)
        full = jnp.concatenate([acc, jnp.broadcast_to(top, (row_count, 128 - HD))], axis=1)
        full = jnp.where(lane128 == HD + 1, total, full)
        for half in range(halves):
            block = jnp.concatenate(
                [
                    full[h * steps + half * n_tok : h * steps + (half + 1) * n_tok]
                    for h in range(heads)
                ],
                axis=0,
            )
            sb[r * halves + half] = pad_rows(block, sb.shape[1])

    s_copies = [
        to_seq(sb.at[lax.rem(me_s + d, ns)], rb.at[d - 1], s_send, s_recv, d)
        for d in range(1, ns)
    ]
    for copy in s_copies:
        copy.start()
    pick_row = lax.broadcasted_iota(jnp.int32, (8, rows), 0)
    pick_col = lax.broadcasted_iota(jnp.int32, (8, rows), 1)
    pick = jnp.where((pick_col == me_s * n_tok + pick_row) & (pick_row < n_tok), 1.0, 0.0)
    own_x = [dot(pick.astype(BF16), xg[c])[:n_tok] for c in range(nt)]
    for copy in s_copies:
        copy.wait()
    parts = [sb[me_s]] + [rb[d] for d in range(ns - 1)]
    top = parts[0][:, HD : HD + 1]
    for part in parts[1:]:
        top = jnp.maximum(top, part[:, HD : HD + 1])
    merged = jnp.zeros_like(parts[0])
    for part in parts:
        merged = merged + part * jnp.exp(part[:, HD : HD + 1] - top)
    attended = merged[:, :HD] / merged[:, HD + 1 : HD + 2]
    attended = jnp.concatenate(
        [attended[h * n_tok : (h + 1) * n_tok] for h in range(heads)], axis=1
    )
    attended = pad_rows(attended, 8).astype(BF16)

    copies[10].wait()
    head_term = dot(attended, wo_v[...])[:n_tok]
    head_parts = [head_term[:, c * dl : (c + 1) * dl] for c in range(nt)]
    ob[...] = pad_rows(jnp.concatenate(head_parts, axis=0), ob.shape[0]).astype(BF16)
    o_copies = [to_tp(ob, orb.at[d - 1], o_send, o_recv, d) for d in range(1, nt)]
    for copy in o_copies:
        copy.start()
    stream = [a + b for a, b in zip(own_x, head_parts)]
    for copy in o_copies:
        copy.wait()
    for d in range(nt - 1):
        got = orb[d].astype(F32)
        stream = [s + got[c * n_tok : (c + 1) * n_tok] for c, s in enumerate(stream)]

    copies[11].wait()
    square = jnp.zeros((n_tok, 1), F32)
    for piece in stream:
        square = square + jnp.sum(piece * piece, axis=-1, keepdims=True)
    inverse = lax.rsqrt(square * np.float32(1.0 / model) + EPS)
    gain = mg_v[...].astype(F32)[None]
    mlp_in = [
        pad_rows(piece * inverse * gain[:, c * dl : (c + 1) * dl], 8).astype(BF16)
        for c, piece in enumerate(stream)
    ]
    for c, piece in enumerate(stream):
        stx[c] = fold(piece, fold_rows)
    copies[12].wait()
    gate = project_t(mlp_in, wg_v)
    copies[13].wait()
    lift = project_t(mlp_in, wu_v)
    hidden = (gate / (1.0 + jnp.exp(-gate)) * lift).astype(BF16)
    copies[14].wait()
    down = dot(hidden, wd_v[...])[:n_tok]
    for c in range(nt):
        db[c] = fold(down[:, c * dl : (c + 1) * dl], fold_rows).astype(BF16)
    d_copies = [
        to_tp(db.at[lax.rem(me_t + d, nt)], drb.at[d - 1], d_send, d_recv, d)
        for d in range(1, nt)
    ]
    for copy in d_copies:
        copy.start()
    result = stx[me_t] + db[me_t].astype(F32)
    for copy in d_copies:
        copy.wait()
    for d in range(nt - 1):
        result = result + drb[d].astype(F32)
    frb[me_s] = result.astype(BF16)

    f_copies = [to_seq(frb.at[me_s], frb.at[me_s], f_send, f_recv, d) for d in range(1, ns)]
    for copy in f_copies:
        copy.start()
    for copy in f_copies:
        copy.wait()
    out[...] = jnp.concatenate(
        [unfold(frb[j].astype(F32), n_tok, dl) for j in range(ns)], axis=0
    ).astype(BF16)


def body(
    ns, nt, tokens_in, attn_gain, mlp_gain, proj_query, proj_key, proj_value, proj_out,
    proj_gate, proj_up, proj_down, long_keys, long_values, short_keys, short_values,
    long_seen, short_len,
):
    steps, reqs, dl = tokens_in.shape
    model, ql = proj_query.shape
    rows = steps * reqs
    n_tok = rows // ns
    index = (np.arange(ql) % HD) % HALF
    freq = (THETA ** (-2.0 * index.astype(np.float64) / HD)).astype(np.float32)[None]
    operands = (
        tokens_in, attn_gain, mlp_gain, proj_query, proj_key.T, proj_value.T,
        proj_out, proj_gate.T, proj_up.T, proj_down, long_keys.transpose(1, 2, 0),
        long_values.transpose(1, 2, 0), short_keys, short_values, jnp.asarray(freq),
    )
    chunk_rows = up_to((ql // HD) * n_tok, 8)
    fold_rows = up_to(-(-dl // 128) * n_tok, 16)
    out_rows = up_to(nt * n_tok, 16)
    dma = pltpu.SemaphoreType.DMA
    out = pl.pallas_call(
        functools.partial(kernel, ns, nt),
        out_shape=jax.ShapeDtypeStruct((rows, dl), BF16),
        in_specs=[pl.BlockSpec(memory_space=pl.ANY)] * len(operands)
        + [pl.BlockSpec(memory_space=pltpu.SMEM)] * 2,
        out_specs=pl.BlockSpec(memory_space=pltpu.VMEM),
        scratch_shapes=[pltpu.VMEM(a.shape, a.dtype) for a in operands]
        + [
            pltpu.VMEM((nt, rows, dl), BF16),
            pltpu.VMEM((ns, chunk_rows, 128), F32),
            pltpu.VMEM((ns - 1, chunk_rows, 128), F32),
            pltpu.VMEM((out_rows, dl), BF16),
            pltpu.VMEM((nt - 1, out_rows, dl), BF16),
            pltpu.VMEM((nt, fold_rows, 128), F32),
            pltpu.VMEM((nt, fold_rows, 128), BF16),
            pltpu.VMEM((nt - 1, fold_rows, 128), BF16),
            pltpu.VMEM((ns, fold_rows, 128), BF16),
            dma((len(operands),)),
            dma((nt - 1,)), dma((nt - 1,)),
            dma((ns - 1,)), dma((ns - 1,)),
            dma((nt - 1,)), dma((nt - 1,)),
            dma((nt - 1,)), dma((nt - 1,)),
            dma((ns - 1,)), dma((ns - 1,)),
        ],
        compiler_params=pltpu.CompilerParams(
            collective_id=0, has_side_effects=True, vmem_limit_bytes=60 * 1024 * 1024
        ),
    )(*operands, long_seen, short_len)
    return out.reshape(reqs, steps, dl).transpose(1, 0, 2)


def solution(mesh):
    ns, nt = mesh.shape["seq"], mesh.shape["tp"]
    in_specs = (
        P(None, None, "tp"),
        P(),
        P(),
        P(None, "tp"),
        P(None, "tp"),
        P(None, "tp"),
        P("tp", None),
        P(None, "tp"),
        P(None, "tp"),
        P("tp", None),
        P("seq", "tp", None),
        P("seq", "tp", None),
        P("seq", "tp", None),
        P("seq", "tp", None),
        P(),
        P(),
    )
    return jax.shard_map(
        functools.partial(body, ns, nt),
        mesh=mesh,
        in_specs=in_specs,
        out_specs=P(None, None, "tp"),
        check_vma=False,
    )
```

```python
import functools
import math

import jax
import jax.numpy as jnp
import numpy as np
from jax import lax
from jax.experimental import pallas as pl
from jax.experimental.pallas import tpu as pltpu
from jax.sharding import PartitionSpec as P

HEADS = 32
KV_HEADS = 8
HD = 80
HALF = HD // 2
GROUP = HEADS // KV_HEADS
WIN = 4096
STEPS = 8

EPS = 1e-05
THETA = 10000.0
HIDDEN_SCORE = -1e30
SCALE = 1.0 / math.sqrt(HD)
F32 = jnp.float32
BF16 = jnp.bfloat16
MESH = pl.DeviceIdType.MESH


def up_to(n, unit):
    return -(-n // unit) * unit


def dot(a, b):
    return lax.dot_general(a, b, (((1,), (0,)), ((), ())), preferred_element_type=F32)


def dot_t(a, b):
    return lax.dot_general(a, b, (((1,), (1,)), ((), ())), preferred_element_type=F32)


def pad_rows(v, rows):
    if v.shape[0] == rows:
        return v
    return jnp.concatenate([v, jnp.zeros((rows - v.shape[0], v.shape[1]), v.dtype)], axis=0)


def iota(shape, axis):
    return lax.broadcasted_iota(jnp.int32, shape, axis)


def one_hot(condition):
    return jnp.where(condition, 1.0, 0.0).astype(BF16)


def sine_cosine(angle):
    turns = jnp.floor(angle * np.float32(2.0 / math.pi) + 0.5)
    rest = angle - turns * np.float32(1.5703125)
    rest = rest - turns * np.float32(4.8351287841796875e-4)
    rest = rest - turns * np.float32(math.pi / 2 - 1.5703125 - 4.8351287841796875e-4)
    sq = rest * rest
    sine = rest + rest * sq * (
        np.float32(-1.6666654611e-1)
        + sq * (np.float32(8.3321608736e-3) + sq * np.float32(-1.9515295891e-4))
    )
    cosine = 1.0 - 0.5 * sq + sq * sq * (
        np.float32(4.166664568298827e-2)
        + sq * (np.float32(-1.388731625493765e-3) + sq * np.float32(2.443315711809948e-5))
    )
    quarter = turns - 4.0 * jnp.floor(turns * 0.25)
    odd = (quarter == 1.0) | (quarter == 3.0)
    sin_out = jnp.where(odd, cosine, sine)
    cos_out = jnp.where(odd, sine, cosine)
    sin_out = jnp.where(quarter >= 2.0, -sin_out, sin_out)
    cos_out = jnp.where((quarter == 1.0) | (quarter == 2.0), -cos_out, cos_out)
    return sin_out, cos_out


def rope(v, cosine, signed_sine, front):
    ahead = jnp.concatenate([v[:, HALF:], v[:, :HALF]], axis=1)
    behind = jnp.concatenate([v[:, -HALF:], v[:, :-HALF]], axis=1)
    return v * cosine + jnp.where(front, ahead, behind) * signed_sine


def kernel(
    ns, nt, tok, ag, mg, wq, wk, wv, wo, wg, wu, wd, lk, lv, sk, sv, fr, seen, slen, out,
    ag_v, mg_v, wq_v, wk_v, wv_v, wo_v, wg_v, wu_v, wd_v, lk_v, lv_v, sk_v, sv_v, fr_v,
    xg, sb, rb, ob, orb, db, drb, fb, local_sem,
    x_send, x_recv, s_send, s_recv, o_send, o_recv, d_send, d_recv, f_send, f_recv,
):
    me_s = lax.axis_index("seq")
    me_t = lax.axis_index("tp")
    steps, reqs, dl = tok.shape
    rows = steps * reqs
    copies_of_step = ns // steps
    my_step = me_s // copies_of_step
    my_twin = lax.rem(me_s, copies_of_step)
    model = wq.shape[0]
    ql = wq.shape[1]
    kl = wk.shape[0]
    heads = ql // HD
    kvl = kl // HD
    long_slots = lk.shape[2]
    short_slots = sk.shape[0]

    barrier = pltpu.get_barrier_semaphore()
    for d in range(1, nt):
        pl.semaphore_signal(
            barrier, inc=1, device_id=(me_s, lax.rem(me_t + d, nt)), device_id_type=MESH
        )
    for d in range(1, ns):
        pl.semaphore_signal(
            barrier, inc=1, device_id=(lax.rem(me_s + d, ns), me_t), device_id_type=MESH
        )

    pairs = [
        (tok, xg.at[me_t]), (ag, ag_v), (fr, fr_v), (wq, wq_v), (wk, wk_v), (wv, wv_v),
        (lk, lk_v), (sk, sk_v), (lv, lv_v), (sv, sv_v), (wo, wo_v), (mg, mg_v),
        (wg, wg_v), (wu, wu_v), (wd, wd_v),
    ]
    copies = []
    for i, (src, dst) in enumerate(pairs):
        copies.append(pltpu.make_async_copy(src, dst, local_sem.at[i]))
        copies[i].start()

    def to_tp(src, dst, send, recv, d):
        return pltpu.make_async_remote_copy(
            src_ref=src, dst_ref=dst, send_sem=send.at[d - 1], recv_sem=recv.at[d - 1],
            device_id=(me_s, lax.rem(me_t + d, nt)), device_id_type=MESH,
        )

    def to_seq(src, dst, send, recv, d, target):
        return pltpu.make_async_remote_copy(
            src_ref=src, dst_ref=dst, send_sem=send.at[d - 1], recv_sem=recv.at[d - 1],
            device_id=(target, me_t), device_id_type=MESH,
        )

    pl.semaphore_wait(barrier, nt - 1 + ns - 1)
    x_copies = [to_tp(tok, xg.at[me_t], x_send, x_recv, d) for d in range(1, nt)]
    for copy in x_copies:
        copy.start()

    copies[2].wait()
    row = iota((rows, 1), 0)
    req = row % reqs
    base = jnp.where(req == 0, seen[0], 0)
    for r in range(1, reqs):
        base = jnp.where(req == r, slen[r - 1], base)
    position = (base + row // reqs).astype(F32)
    sine, cosine = sine_cosine(position * fr_v[...])
    front = iota((rows, ql), 1) % HD < HALF
    signed_sine = jnp.where(front, -sine, sine)
    q_rows, k_rows, m_rows = rows * heads, rows * kvl, reqs * heads
    i = iota((q_rows, 1), 0)
    order_q = one_hot(
        iota((q_rows, q_rows), 1)
        == (i % heads) * rows + (i // heads % steps) * reqs + i // (heads * steps)
    )
    i = iota((k_rows, 1), 0)
    order_k = one_hot(
        iota((k_rows, k_rows), 1)
        == (i // steps % kvl) * rows + (i % steps) * reqs + i // (steps * kvl)
    )
    lane128 = iota((128, 128), 0)
    spread_top = one_hot((lane128 >= HD) & (lane128 < HD + 3))
    spread_heads = one_hot(iota((HD, ql), 1) % HD == iota((HD, ql), 0))
    own_head = iota((m_rows, ql), 1) // HD == iota((m_rows, ql), 0) % heads
    join_heads = one_hot(iota((8, m_rows), 1) // heads == iota((8, m_rows), 0))

    for copy in x_copies:
        copy.wait()
    copies[0].wait()
    copies[1].wait()
    pieces = [xg[c].astype(F32).reshape(rows, dl) for c in range(nt)]
    square = jnp.zeros((rows, 1), F32)
    for piece in pieces:
        square = square + jnp.sum(piece * piece, axis=-1, keepdims=True)
    inverse = lax.rsqrt(square * np.float32(1.0 / model) + EPS)
    gain = ag_v[...].astype(F32)[None]
    normed = [
        (piece * inverse * gain[:, c * dl : (c + 1) * dl]).astype(BF16)
        for c, piece in enumerate(pieces)
    ]

    def project(parts, weight):
        total = None
        for c, part in enumerate(parts):
            term = dot(part, weight[c * dl : (c + 1) * dl, :])
            total = term if total is None else total + term
        return total

    def project_t(parts, weight):
        total = None
        for c, part in enumerate(parts):
            term = dot_t(part, weight[:, c * dl : (c + 1) * dl])
            total = term if total is None else total + term
        return total

    def stack(v, count):
        return jnp.concatenate([v[:, k * HD : (k + 1) * HD] for k in range(count)], axis=0)

    copies[4].wait()
    copies[5].wait()
    copies[3].wait()
    key = rope(project_t(normed, wk_v), cosine[:, :kl], signed_sine[:, :kl], front[:, :kl])
    value = project_t(normed, wv_v)
    query = rope(project(normed, wq_v), cosine, signed_sine, front)
    key = dot(order_k, stack(key, kvl).astype(BF16))
    value = dot(order_k, stack(value, kvl).astype(BF16))
    query = dot(order_q, stack(query, heads).astype(BF16))

    for n in (6, 7, 8, 9):
        copies[n].wait()
    short_k = sk_v[...].reshape(short_slots * kvl, sk.shape[2])
    short_v = sv_v[...].reshape(short_slots * kvl, sv.shape[2])
    row_count = heads * steps
    new_count = kvl * steps
    i = iota((row_count, 1), 0)
    step_of = i // heads
    kv_of = i % heads // GROUP
    new_col = iota((1, new_count), 1)
    new_mask = (kv_of == new_col // steps) & (new_col % steps <= step_of) & (me_s == 0)
    lane = iota((row_count, 128), 1)

    def by_kv(terms):
        total = terms[0]
        for k in range(1, kvl):
            total = jnp.where(kv_of == k, terms[k], total)
        return total

    blocks = []
    for r in range(reqs):
        q_r = query[r * row_count : (r + 1) * row_count].astype(BF16)
        k_r = key[r * new_count : (r + 1) * new_count].astype(BF16)
        v_r = value[r * new_count : (r + 1) * new_count].astype(BF16)
        if r == 0:
            slot = me_s * long_slots + iota((1, long_slots), 1)
            old_mask = ((slot - seen[0]) & (WIN - 1)) > step_of
            old_dots = by_kv([dot(q_r, lk_v[k]) for k in range(kvl)])
        else:
            cut = slice((r - 1) * HD, r * HD)
            col = iota((1, short_slots * kvl), 1)
            slot = me_s * short_slots + col // kvl
            old_mask = (kv_of == col % kvl) & (slot < slen[r - 1])
            old_dots = dot_t(q_r, short_k[:, cut])
        old_score = jnp.where(old_mask, old_dots * SCALE, HIDDEN_SCORE)
        new_score = jnp.where(new_mask, dot_t(q_r, k_r) * SCALE, HIDDEN_SCORE)
        top = jnp.maximum(
            jnp.max(old_score, axis=-1, keepdims=True), jnp.max(new_score, axis=-1, keepdims=True)
        )
        old_w = jnp.where(old_mask, jnp.exp(old_score - top), 0.0)
        new_w = jnp.where(new_mask, jnp.exp(new_score - top), 0.0)
        total = jnp.sum(old_w, axis=-1, keepdims=True) + jnp.sum(new_w, axis=-1, keepdims=True)
        old_w = old_w.astype(BF16)
        if r == 0:
            acc = by_kv([dot_t(old_w, lv_v[k]) for k in range(kvl)])
        else:
            acc = dot(old_w, short_v[:, cut])
        acc = acc + dot(new_w.astype(BF16), v_r)
        full = jnp.concatenate([acc, jnp.zeros((row_count, 128 - HD), F32)], axis=1)
        terms = []
        for number, count in ((top, 3), (total, 2)):
            rest = number
            for _ in range(count):
                term = rest.astype(BF16).astype(F32)
                terms.append(term)
                rest = rest - term
        for n, term in enumerate(terms):
            full = jnp.where(lane == HD + n, term, full)
        blocks.append(full)
    for t in range(steps):
        sb[t] = jnp.concatenate(
            [full[t * heads : (t + 1) * heads] for full in blocks], axis=0
        ).astype(BF16)

    s_copies = []
    for d in range(1, ns):
        target = lax.rem(me_s + d, ns)
        s_copies.append(
            to_seq(sb.at[target // copies_of_step], rb.at[d - 1], s_send, s_recv, d, target)
        )
    for copy in s_copies:
        copy.start()
    stream = [xg[c, my_step].astype(F32) for c in range(nt)]
    for copy in s_copies:
        copy.wait()
    parts = [sb[my_step]] + [rb[d] for d in range(ns - 1)]
    tops = [dot(part, spread_top) for part in parts]
    top = functools.reduce(jnp.maximum, tops)
    merged = jnp.zeros((m_rows, 128), F32)
    for part, part_top in zip(parts, tops):
        merged = merged + part.astype(F32) * jnp.exp(part_top - top)
    attended = merged[:, :HD] / (merged[:, HD + 3 : HD + 4] + merged[:, HD + 4 : HD + 5])
    attended = jnp.where(own_head, dot(attended.astype(BF16), spread_heads), 0.0).astype(BF16)
    attended = dot(join_heads, attended).astype(BF16)

    copies[10].wait()
    head_term = dot(attended, wo_v[...])[:reqs]
    head_parts = [head_term[:, c * dl : (c + 1) * dl] for c in range(nt)]
    ob[...] = jnp.concatenate(head_parts, axis=0).astype(BF16)
    o_copies = [to_tp(ob, orb.at[d - 1], o_send, o_recv, d) for d in range(1, nt)]
    for copy in o_copies:
        copy.start()
    stream = [a + b for a, b in zip(stream, head_parts)]
    copies[11].wait()
    gain = mg_v[...].astype(F32)[None]
    for copy in o_copies:
        copy.wait()
    got = orb[0].astype(F32)
    for d in range(1, nt - 1):
        got = got + orb[d].astype(F32)
    stream = [s + got[c * reqs : (c + 1) * reqs] for c, s in enumerate(stream)]
    square = jnp.zeros((reqs, 1), F32)
    for piece in stream:
        square = square + jnp.sum(piece * piece, axis=-1, keepdims=True)
    inverse = lax.rsqrt(square * np.float32(1.0 / model) + EPS)
    mlp_in = [
        pad_rows(piece * inverse * gain[:, c * dl : (c + 1) * dl], 8).astype(BF16)
        for c, piece in enumerate(stream)
    ]
    copies[12].wait()
    gate = project_t(mlp_in, wg_v)
    copies[13].wait()
    lift = project_t(mlp_in, wu_v)
    hidden = (gate / (1.0 + jnp.exp(-gate)) * lift).astype(BF16)
    copies[14].wait()
    down = dot(hidden, wd_v[...])[:reqs]
    result = jnp.zeros((reqs, dl), F32)
    for c in range(nt):
        piece = down[:, c * dl : (c + 1) * dl]
        db[c] = piece.astype(BF16)
        result = result + jnp.where(me_t == c, stream[c] + piece, 0.0)
    d_copies = [
        to_tp(db.at[lax.rem(me_t + d, nt)], drb.at[d - 1], d_send, d_recv, d)
        for d in range(1, nt)
    ]
    for copy in d_copies:
        copy.start()
    for copy in d_copies:
        copy.wait()
    for d in range(nt - 1):
        result = result + drb[d].astype(F32)
    fb[...] = result.astype(BF16)

    f_copies = []
    for d in range(1, steps):
        target = lax.rem(my_step + d, steps) * copies_of_step + my_twin
        f_copies.append(to_seq(fb, out.at[my_step], f_send, f_recv, d, target))
    for copy in f_copies:
        copy.start()
    own = pltpu.make_async_copy(fb, out.at[my_step], local_sem.at[len(pairs)])
    own.start()
    for copy in f_copies:
        copy.wait()
    own.wait()


def body(
    ns, nt, tokens_in, attn_gain, mlp_gain, proj_query, proj_key, proj_value, proj_out,
    proj_gate, proj_up, proj_down, long_keys, long_values, short_keys, short_values,
    long_seen, short_len,
):
    steps, reqs, dl = tokens_in.shape
    ql = proj_query.shape[1]
    rows = steps * reqs
    m_rows = reqs * (ql // HD)
    index = (np.arange(ql) % HD) % HALF
    freq = (THETA ** (-2.0 * index.astype(np.float64) / HD)).astype(np.float32)[None]
    operands = (
        tokens_in, attn_gain, mlp_gain, proj_query, proj_key.T, proj_value.T,
        proj_out, proj_gate.T, proj_up.T, proj_down, long_keys.transpose(1, 2, 0),
        long_values.transpose(1, 2, 0), short_keys, short_values, jnp.asarray(freq),
    )
    dma = pltpu.SemaphoreType.DMA
    return pl.pallas_call(
        functools.partial(kernel, ns, nt),
        out_shape=jax.ShapeDtypeStruct(tokens_in.shape, BF16),
        in_specs=[pl.BlockSpec(memory_space=pl.ANY)] * len(operands)
        + [pl.BlockSpec(memory_space=pltpu.SMEM)] * 2,
        out_specs=pl.BlockSpec(memory_space=pl.ANY),
        scratch_shapes=[pltpu.VMEM(a.shape, a.dtype) for a in operands[1:]]
        + [
            pltpu.VMEM((nt, steps, reqs, dl), BF16),
            pltpu.VMEM((steps, m_rows, 128), BF16),
            pltpu.VMEM((ns - 1, m_rows, 128), BF16),
            pltpu.VMEM((nt * reqs, dl), BF16),
            pltpu.VMEM((nt - 1, nt * reqs, dl), BF16),
            pltpu.VMEM((nt, reqs, dl), BF16),
            pltpu.VMEM((nt - 1, reqs, dl), BF16),
            pltpu.VMEM((reqs, dl), BF16),
            dma((len(operands) + 1,)),
            dma((nt - 1,)), dma((nt - 1,)),
            dma((ns - 1,)), dma((ns - 1,)),
            dma((nt - 1,)), dma((nt - 1,)),
            dma((nt - 1,)), dma((nt - 1,)),
            dma((steps - 1,)), dma((steps - 1,)),
        ],
        compiler_params=pltpu.CompilerParams(
            collective_id=0, has_side_effects=True, vmem_limit_bytes=60 * 1024 * 1024
        ),
    )(*operands, long_seen, short_len)


def solution(mesh):
    ns, nt = mesh.shape["seq"], mesh.shape["tp"]
    in_specs = (
        P(None, None, "tp"),
        P(),
        P(),
        P(None, "tp"),
        P(None, "tp"),
        P(None, "tp"),
        P("tp", None),
        P(None, "tp"),
        P(None, "tp"),
        P("tp", None),
        P("seq", "tp", None),
        P("seq", "tp", None),
        P("seq", "tp", None),
        P("seq", "tp", None),
        P(),
        P(),
    )
    return jax.shard_map(
        functools.partial(body, ns, nt),
        mesh=mesh,
        in_specs=in_specs,
        out_specs=P(None, None, "tp"),
        check_vma=False,
    )
```

```python
import functools
import math

import jax
import jax.numpy as jnp
import numpy as np
from jax import lax
from jax.experimental import pallas as pl
from jax.experimental.pallas import tpu as pltpu
from jax.sharding import PartitionSpec as P

HEADS = 32
KV_HEADS = 8
HD = 80
HALF = HD // 2
GROUP = HEADS // KV_HEADS
WIN = 4096
STEPS = 8

EPS = 1e-05
THETA = 10000.0
HIDDEN_SCORE = -1e30
SCALE = 1.0 / math.sqrt(HD)
F32 = jnp.float32
BF16 = jnp.bfloat16
MESH = pl.DeviceIdType.MESH


def dot(a, b):
    return lax.dot_general(a, b, (((1,), (0,)), ((), ())), preferred_element_type=F32)


def dot_t(a, b):
    return lax.dot_general(a, b, (((1,), (1,)), ((), ())), preferred_element_type=F32)


def pad_rows(v, rows):
    if v.shape[0] == rows:
        return v
    return jnp.concatenate([v, jnp.zeros((rows - v.shape[0], v.shape[1]), v.dtype)], axis=0)


def iota(shape, axis):
    return lax.broadcasted_iota(jnp.int32, shape, axis)


def one_hot(condition):
    return jnp.where(condition, 1.0, 0.0).astype(BF16)


def sine_cosine(angle):
    turns = jnp.floor(angle * np.float32(2.0 / math.pi) + 0.5)
    rest = angle - turns * np.float32(1.5703125)
    rest = rest - turns * np.float32(4.8351287841796875e-4)
    rest = rest - turns * np.float32(math.pi / 2 - 1.5703125 - 4.8351287841796875e-4)
    sq = rest * rest
    sine = rest + rest * sq * (
        np.float32(-1.6666654611e-1)
        + sq * (np.float32(8.3321608736e-3) + sq * np.float32(-1.9515295891e-4))
    )
    cosine = 1.0 - 0.5 * sq + sq * sq * (
        np.float32(4.166664568298827e-2)
        + sq * (np.float32(-1.388731625493765e-3) + sq * np.float32(2.443315711809948e-5))
    )
    quarter = turns - 4.0 * jnp.floor(turns * 0.25)
    odd = (quarter == 1.0) | (quarter == 3.0)
    sin_out = jnp.where(odd, cosine, sine)
    cos_out = jnp.where(odd, sine, cosine)
    sin_out = jnp.where(quarter >= 2.0, -sin_out, sin_out)
    cos_out = jnp.where((quarter == 1.0) | (quarter == 2.0), -cos_out, cos_out)
    return sin_out, cos_out


def rope(v, cosine, signed_sine, front):
    ahead = jnp.concatenate([v[:, HALF:], v[:, :HALF]], axis=1)
    behind = jnp.concatenate([v[:, -HALF:], v[:, :-HALF]], axis=1)
    return v * cosine + jnp.where(front, ahead, behind) * signed_sine


def kernel(
    ns, nt, tok, ag, mg, wq, wk, wv, wo, wg, wu, wd, lk, lv, sk, sv, fr, seen, slen, out,
    ag_v, mg_v, wq_v, wk_v, wv_v, wo_v, wg_v, wu_v, wd_v, lk_v, lv_v, sk_v, sv_v, fr_v,
    xg, sb, rb, ob, orb, db, drb, fb, local_sem,
    x_send, x_recv, s_send, s_recv, o_send, o_recv, d_send, d_recv, f_send, f_recv,
):
    me_s = lax.axis_index("seq")
    me_t = lax.axis_index("tp")
    steps, reqs, dl = tok.shape
    rows = steps * reqs
    copies_of_step = ns // steps
    my_step = me_s // copies_of_step
    my_twin = lax.rem(me_s, copies_of_step)
    model = wq.shape[0]
    ql = wq.shape[1]
    kl = wk.shape[0]
    heads = ql // HD
    kvl = kl // HD
    long_slots = lk.shape[2]
    short_slots = sk.shape[0]

    barrier = pltpu.get_barrier_semaphore()
    for d in range(1, nt):
        pl.semaphore_signal(
            barrier, inc=1, device_id=(me_s, lax.rem(me_t + d, nt)), device_id_type=MESH
        )
    for d in range(1, ns):
        pl.semaphore_signal(
            barrier, inc=1, device_id=(lax.rem(me_s + d, ns), me_t), device_id_type=MESH
        )

    def load(n, src, dst):
        return pltpu.make_async_copy(src, dst, local_sem.at[n])

    first = [
        load(0, wk, wk_v), load(1, wv, wv_v), load(2, fr, fr_v), load(3, ag, ag_v),
        load(4, tok, xg.at[me_t]),
    ]
    first += [
        load(5 + c, wq.at[pl.ds(c * dl, dl)], wq_v.at[pl.ds(c * dl, dl)]) for c in range(nt)
    ]
    cached = [
        load(5 + nt + n, src, dst)
        for n, (src, dst) in enumerate([(lk, lk_v), (sk, sk_v), (lv, lv_v), (sv, sv_v)])
    ]
    later = [
        load(9 + nt + n, src, dst)
        for n, (src, dst) in enumerate(
            [(mg, mg_v), (wo, wo_v), (wg, wg_v), (wu, wu_v), (wd, wd_v)]
        )
    ]
    for copy in first + cached:
        copy.start()

    def to_tp(src, dst, send, recv, d):
        return pltpu.make_async_remote_copy(
            src_ref=src, dst_ref=dst, send_sem=send.at[d - 1], recv_sem=recv.at[d - 1],
            device_id=(me_s, lax.rem(me_t + d, nt)), device_id_type=MESH,
        )

    def to_seq(src, dst, send, recv, d, target):
        return pltpu.make_async_remote_copy(
            src_ref=src, dst_ref=dst, send_sem=send.at[d - 1], recv_sem=recv.at[d - 1],
            device_id=(target, me_t), device_id_type=MESH,
        )

    pl.semaphore_wait(barrier, nt - 1 + ns - 1)
    x_copies = [to_tp(tok, xg.at[me_t], x_send, x_recv, d) for d in range(1, nt)]
    for copy in x_copies:
        copy.start()

    first[2].wait()
    row = iota((rows, 1), 0)
    req = row % reqs
    base = jnp.where(req == 0, seen[0], 0)
    for r in range(1, reqs):
        base = jnp.where(req == r, slen[r - 1], base)
    position = (base + row // reqs).astype(F32)
    sine, cosine = sine_cosine(position * fr_v[...])
    front = iota((rows, ql), 1) % HD < HALF
    signed_sine = jnp.where(front, -sine, sine)
    q_rows, k_rows, m_rows = rows * heads, rows * kvl, reqs * heads
    i = iota((q_rows, 1), 0)
    order_q = one_hot(
        iota((q_rows, q_rows), 1)
        == (i % heads) * rows + (i // heads % steps) * reqs + i // (heads * steps)
    )
    i = iota((k_rows, 1), 0)
    order_k = one_hot(
        iota((k_rows, k_rows), 1)
        == (i // steps % kvl) * rows + (i % steps) * reqs + i // (steps * kvl)
    )
    lane128 = iota((128, 128), 0)
    spread_top = one_hot((lane128 >= HD) & (lane128 < HD + 3))
    spread_heads = one_hot(iota((HD, ql), 1) % HD == iota((HD, ql), 0))
    own_head = iota((m_rows, ql), 1) // HD == iota((m_rows, ql), 0) % heads
    join_heads = one_hot(iota((8, m_rows), 1) // heads == iota((8, m_rows), 0))

    for n, copy in enumerate(first + cached):
        if n != 2:
            copy.wait()
    for copy in later:
        copy.start()
    for copy in x_copies:
        copy.wait()
    pieces = [xg[c].astype(F32).reshape(rows, dl) for c in range(nt)]
    square = jnp.zeros((rows, 1), F32)
    for piece in pieces:
        square = square + jnp.sum(piece * piece, axis=-1, keepdims=True)
    inverse = lax.rsqrt(square * np.float32(1.0 / model) + EPS)
    gain = ag_v[...].astype(F32)[None]
    normed = [
        (piece * inverse * gain[:, c * dl : (c + 1) * dl]).astype(BF16)
        for c, piece in enumerate(pieces)
    ]

    def project(parts, weight):
        total = None
        for c, part in enumerate(parts):
            term = dot(part, weight[c * dl : (c + 1) * dl, :])
            total = term if total is None else total + term
        return total

    def project_t(parts, weight):
        total = None
        for c, part in enumerate(parts):
            term = dot_t(part, weight[:, c * dl : (c + 1) * dl])
            total = term if total is None else total + term
        return total

    def stack(v, count):
        return jnp.concatenate([v[:, k * HD : (k + 1) * HD] for k in range(count)], axis=0)

    key = rope(project_t(normed, wk_v), cosine[:, :kl], signed_sine[:, :kl], front[:, :kl])
    value = project_t(normed, wv_v)
    query = rope(project(normed, wq_v), cosine, signed_sine, front)
    key = dot(order_k, stack(key, kvl).astype(BF16))
    value = dot(order_k, stack(value, kvl).astype(BF16))
    query = dot(order_q, stack(query, heads).astype(BF16))

    short_k = sk_v[...].reshape(short_slots * kvl, sk.shape[2])
    short_v = sv_v[...].reshape(short_slots * kvl, sv.shape[2])
    row_count = heads * steps
    new_count = kvl * steps
    i = iota((row_count, 1), 0)
    step_of = i // heads
    kv_of = i % heads // GROUP
    new_col = iota((1, new_count), 1)
    new_mask = (kv_of == new_col // steps) & (new_col % steps <= step_of) & (me_s == 0)
    lane = iota((row_count, 128), 1)

    def by_kv(terms):
        total = terms[0]
        for k in range(1, kvl):
            total = jnp.where(kv_of == k, terms[k], total)
        return total

    blocks = []
    for r in range(reqs):
        q_r = query[r * row_count : (r + 1) * row_count].astype(BF16)
        k_r = key[r * new_count : (r + 1) * new_count].astype(BF16)
        v_r = value[r * new_count : (r + 1) * new_count].astype(BF16)
        if r == 0:
            slot = me_s * long_slots + iota((1, long_slots), 1)
            old_mask = ((slot - seen[0]) & (WIN - 1)) > step_of
            old_dots = by_kv([dot(q_r, lk_v[k]) for k in range(kvl)])
        else:
            cut = slice((r - 1) * HD, r * HD)
            col = iota((1, short_slots * kvl), 1)
            slot = me_s * short_slots + col // kvl
            old_mask = (kv_of == col % kvl) & (slot < slen[r - 1])
            old_dots = dot_t(q_r, short_k[:, cut])
        old_score = jnp.where(old_mask, old_dots * SCALE, HIDDEN_SCORE)
        new_score = jnp.where(new_mask, dot_t(q_r, k_r) * SCALE, HIDDEN_SCORE)
        top = jnp.maximum(
            jnp.max(old_score, axis=-1, keepdims=True), jnp.max(new_score, axis=-1, keepdims=True)
        )
        old_w = jnp.where(old_mask, jnp.exp(old_score - top), 0.0)
        new_w = jnp.where(new_mask, jnp.exp(new_score - top), 0.0)
        total = jnp.sum(old_w, axis=-1, keepdims=True) + jnp.sum(new_w, axis=-1, keepdims=True)
        old_w = old_w.astype(BF16)
        if r == 0:
            acc = by_kv([dot_t(old_w, lv_v[k]) for k in range(kvl)])
        else:
            acc = dot(old_w, short_v[:, cut])
        acc = acc + dot(new_w.astype(BF16), v_r)
        full = jnp.concatenate([acc, jnp.zeros((row_count, 128 - HD), F32)], axis=1)
        terms = []
        for number, count in ((top, 3), (total, 2)):
            rest = number
            for _ in range(count):
                term = rest.astype(BF16).astype(F32)
                terms.append(term)
                rest = rest - term
        for n, term in enumerate(terms):
            full = jnp.where(lane == HD + n, term, full)
        blocks.append(full)
    for t in range(steps):
        sb[t] = jnp.concatenate(
            [full[t * heads : (t + 1) * heads] for full in blocks], axis=0
        ).astype(BF16)

    s_copies = []
    for d in range(1, ns):
        target = lax.rem(me_s + d, ns)
        s_copies.append(
            to_seq(sb.at[target // copies_of_step], rb.at[d - 1], s_send, s_recv, d, target)
        )
    for copy in s_copies:
        copy.start()
    stream = [xg[c, my_step].astype(F32) for c in range(nt)]
    for copy in s_copies:
        copy.wait()
    parts = [sb[my_step]] + [rb[d] for d in range(ns - 1)]
    tops = [dot(part, spread_top) for part in parts]
    top = functools.reduce(jnp.maximum, tops)
    merged = jnp.zeros((m_rows, 128), F32)
    for part, part_top in zip(parts, tops):
        merged = merged + part.astype(F32) * jnp.exp(part_top - top)
    attended = merged[:, :HD] / (merged[:, HD + 3 : HD + 4] + merged[:, HD + 4 : HD + 5])
    attended = jnp.where(own_head, dot(attended.astype(BF16), spread_heads), 0.0).astype(BF16)
    attended = dot(join_heads, attended).astype(BF16)

    later[1].wait()
    head_term = dot(attended, wo_v[...])[:reqs]
    head_parts = [head_term[:, c * dl : (c + 1) * dl] for c in range(nt)]
    ob[...] = jnp.concatenate(head_parts, axis=0).astype(BF16)
    o_copies = [to_tp(ob, orb.at[d - 1], o_send, o_recv, d) for d in range(1, nt)]
    for copy in o_copies:
        copy.start()
    stream = [a + b for a, b in zip(stream, head_parts)]
    later[0].wait()
    gain = mg_v[...].astype(F32)[None]
    for copy in o_copies:
        copy.wait()
    got = orb[0].astype(F32)
    for d in range(1, nt - 1):
        got = got + orb[d].astype(F32)
    stream = [s + got[c * reqs : (c + 1) * reqs] for c, s in enumerate(stream)]
    square = jnp.zeros((reqs, 1), F32)
    for piece in stream:
        square = square + jnp.sum(piece * piece, axis=-1, keepdims=True)
    inverse = lax.rsqrt(square * np.float32(1.0 / model) + EPS)
    mlp_in = [
        pad_rows(piece * inverse * gain[:, c * dl : (c + 1) * dl], 8).astype(BF16)
        for c, piece in enumerate(stream)
    ]
    later[2].wait()
    gate = project_t(mlp_in, wg_v)
    later[3].wait()
    lift = project_t(mlp_in, wu_v)
    hidden = (gate / (1.0 + jnp.exp(-gate)) * lift).astype(BF16)
    later[4].wait()
    down = dot(hidden, wd_v[...])[:reqs]
    result = jnp.zeros((reqs, dl), F32)
    for c in range(nt):
        piece = down[:, c * dl : (c + 1) * dl]
        db[c] = piece.astype(BF16)
        result = result + jnp.where(me_t == c, stream[c] + piece, 0.0)
    d_copies = [
        to_tp(db.at[lax.rem(me_t + d, nt)], drb.at[d - 1], d_send, d_recv, d)
        for d in range(1, nt)
    ]
    for copy in d_copies:
        copy.start()
    for copy in d_copies:
        copy.wait()
    for d in range(nt - 1):
        result = result + drb[d].astype(F32)
    fb[...] = result.astype(BF16)

    f_copies = []
    for d in range(1, steps):
        target = lax.rem(my_step + d, steps) * copies_of_step + my_twin
        f_copies.append(to_seq(fb, out.at[my_step], f_send, f_recv, d, target))
    for copy in f_copies:
        copy.start()
    own = pltpu.make_async_copy(fb, out.at[my_step], local_sem.at[14 + nt])
    own.start()
    for copy in f_copies:
        copy.wait()
    own.wait()


def body(
    ns, nt, tokens_in, attn_gain, mlp_gain, proj_query, proj_key, proj_value, proj_out,
    proj_gate, proj_up, proj_down, long_keys, long_values, short_keys, short_values,
    long_seen, short_len,
):
    steps, reqs, dl = tokens_in.shape
    ql = proj_query.shape[1]
    rows = steps * reqs
    m_rows = reqs * (ql // HD)
    index = (np.arange(ql) % HD) % HALF
    freq = (THETA ** (-2.0 * index.astype(np.float64) / HD)).astype(np.float32)[None]
    operands = (
        tokens_in, attn_gain, mlp_gain, proj_query, proj_key.T, proj_value.T,
        proj_out, proj_gate.T, proj_up.T, proj_down, long_keys.transpose(1, 2, 0),
        long_values.transpose(1, 2, 0), short_keys, short_values, jnp.asarray(freq),
    )
    dma = pltpu.SemaphoreType.DMA
    return pl.pallas_call(
        functools.partial(kernel, ns, nt),
        out_shape=jax.ShapeDtypeStruct(tokens_in.shape, BF16),
        in_specs=[pl.BlockSpec(memory_space=pl.ANY)] * len(operands)
        + [pl.BlockSpec(memory_space=pltpu.SMEM)] * 2,
        out_specs=pl.BlockSpec(memory_space=pl.ANY),
        scratch_shapes=[pltpu.VMEM(a.shape, a.dtype) for a in operands[1:]]
        + [
            pltpu.VMEM((nt, steps, reqs, dl), BF16),
            pltpu.VMEM((steps, m_rows, 128), BF16),
            pltpu.VMEM((ns - 1, m_rows, 128), BF16),
            pltpu.VMEM((nt * reqs, dl), BF16),
            pltpu.VMEM((nt - 1, nt * reqs, dl), BF16),
            pltpu.VMEM((nt, reqs, dl), BF16),
            pltpu.VMEM((nt - 1, reqs, dl), BF16),
            pltpu.VMEM((reqs, dl), BF16),
            dma((15 + nt,)),
            dma((nt - 1,)), dma((nt - 1,)),
            dma((ns - 1,)), dma((ns - 1,)),
            dma((nt - 1,)), dma((nt - 1,)),
            dma((nt - 1,)), dma((nt - 1,)),
            dma((steps - 1,)), dma((steps - 1,)),
        ],
        compiler_params=pltpu.CompilerParams(
            collective_id=0, has_side_effects=True, vmem_limit_bytes=60 * 1024 * 1024
        ),
    )(*operands, long_seen, short_len)


def solution(mesh):
    ns, nt = mesh.shape["seq"], mesh.shape["tp"]
    in_specs = (
        P(None, None, "tp"),
        P(),
        P(),
        P(None, "tp"),
        P(None, "tp"),
        P(None, "tp"),
        P("tp", None),
        P(None, "tp"),
        P(None, "tp"),
        P("tp", None),
        P("seq", "tp", None),
        P("seq", "tp", None),
        P("seq", "tp", None),
        P("seq", "tp", None),
        P(),
        P(),
    )
    return jax.shard_map(
        functools.partial(body, ns, nt),
        mesh=mesh,
        in_specs=in_specs,
        out_specs=P(None, None, "tp"),
        check_vma=False,
    )
```

```python
import functools
import math

import jax
import jax.numpy as jnp
import numpy as np
from jax import lax
from jax.experimental import pallas as pl
from jax.experimental.pallas import tpu as pltpu
from jax.sharding import PartitionSpec as P

HEADS = 32
KV_HEADS = 8
HD = 80
HALF = HD // 2
GROUP = HEADS // KV_HEADS
WIN = 4096
STEPS = 8

EPS = 1e-05
THETA = 10000.0
HIDDEN_SCORE = -1e30
SCALE = 1.0 / math.sqrt(HD)
F32 = jnp.float32
BF16 = jnp.bfloat16
MESH = pl.DeviceIdType.MESH


def dot(a, b):
    return lax.dot_general(a, b, (((1,), (0,)), ((), ())), preferred_element_type=F32)


def dot_t(a, b):
    return lax.dot_general(a, b, (((1,), (1,)), ((), ())), preferred_element_type=F32)


def pad_rows(v, rows):
    if v.shape[0] == rows:
        return v
    return jnp.concatenate([v, jnp.zeros((rows - v.shape[0], v.shape[1]), v.dtype)], axis=0)


def iota(shape, axis):
    return lax.broadcasted_iota(jnp.int32, shape, axis)


def one_hot(condition):
    return jnp.where(condition, 1.0, 0.0).astype(BF16)


def sine_cosine(angle):
    turns = jnp.floor(angle * np.float32(2.0 / math.pi) + 0.5)
    rest = angle - turns * np.float32(1.5703125)
    rest = rest - turns * np.float32(4.8351287841796875e-4)
    rest = rest - turns * np.float32(math.pi / 2 - 1.5703125 - 4.8351287841796875e-4)
    sq = rest * rest
    sine = rest + rest * sq * (
        np.float32(-1.6666654611e-1)
        + sq * (np.float32(8.3321608736e-3) + sq * np.float32(-1.9515295891e-4))
    )
    cosine = 1.0 - 0.5 * sq + sq * sq * (
        np.float32(4.166664568298827e-2)
        + sq * (np.float32(-1.388731625493765e-3) + sq * np.float32(2.443315711809948e-5))
    )
    quarter = turns - 4.0 * jnp.floor(turns * 0.25)
    odd = (quarter == 1.0) | (quarter == 3.0)
    sin_out = jnp.where(odd, cosine, sine)
    cos_out = jnp.where(odd, sine, cosine)
    sin_out = jnp.where(quarter >= 2.0, -sin_out, sin_out)
    cos_out = jnp.where((quarter == 1.0) | (quarter == 2.0), -cos_out, cos_out)
    return sin_out, cos_out


def rope(v, cosine, signed_sine, front):
    ahead = jnp.concatenate([v[:, HALF:], v[:, :HALF]], axis=1)
    behind = jnp.concatenate([v[:, -HALF:], v[:, :-HALF]], axis=1)
    return v * cosine + jnp.where(front, ahead, behind) * signed_sine


def kernel(
    ns, nt, tok, ag, mg, wq, wk, wv, wo, wg, wu, wd, lk, lv, sk, sv, fr, seen, slen, out,
    ag_v, mg_v, wq_v, wk_v, wv_v, wo_v, wg_v, wu_v, wd_v, lk_v, lv_v, sk_v, sv_v, fr_v,
    xg, sb, rb, ob, orb, db, drb, fb, local_sem,
    x_send, x_recv, s_send, s_recv, o_send, o_recv, d_send, d_recv, f_send, f_recv,
):
    me_s = lax.axis_index("seq")
    me_t = lax.axis_index("tp")
    steps, reqs, dl = tok.shape
    rows = steps * reqs
    copies_of_step = ns // steps
    my_step = me_s // copies_of_step
    my_twin = lax.rem(me_s, copies_of_step)
    half = lax.rem(my_step, 2)
    mate_step = my_step + 1 - 2 * half
    mate = mate_step * copies_of_step + my_twin
    ff, share = wd.shape[0], wd_v.shape[0]
    low = pl.multiple_of(half * (ff - share), 16)
    model = wq.shape[0]
    ql = wq.shape[1]
    kl = wk.shape[0]
    heads = ql // HD
    kvl = kl // HD
    long_slots = lk.shape[2]
    short_slots = sk.shape[0]

    barrier = pltpu.get_barrier_semaphore()
    for d in range(1, nt):
        pl.semaphore_signal(
            barrier, inc=1, device_id=(me_s, lax.rem(me_t + d, nt)), device_id_type=MESH
        )
    for d in range(1, ns):
        pl.semaphore_signal(
            barrier, inc=1, device_id=(lax.rem(me_s + d, ns), me_t), device_id_type=MESH
        )

    for d in range(1, nt):
        pl.semaphore_signal(
            barrier, inc=1, device_id=(mate, lax.rem(me_t + d, nt)), device_id_type=MESH
        )

    def load(n, src, dst):
        return pltpu.make_async_copy(src, dst, local_sem.at[n])

    first = [
        load(0, wk, wk_v), load(1, wv, wv_v), load(2, fr, fr_v), load(3, ag, ag_v),
        load(4, tok, xg.at[me_t]),
    ]
    first += [
        load(5 + c, wq.at[pl.ds(c * dl, dl)], wq_v.at[pl.ds(c * dl, dl)]) for c in range(nt)
    ]
    cached = [
        load(5 + nt + n, src, dst)
        for n, (src, dst) in enumerate([(lk, lk_v), (sk, sk_v), (lv, lv_v), (sv, sv_v)])
    ]
    later = [
        load(9 + nt + n, src, dst)
        for n, (src, dst) in enumerate(
            [
                (mg, mg_v),
                (wo, wo_v),
                (wg.at[pl.ds(low, share)], wg_v),
                (wu.at[pl.ds(low, share)], wu_v),
                (wd.at[pl.ds(low, share)], wd_v),
            ]
        )
    ]
    for copy in first + cached:
        copy.start()

    def to_tp(src, dst, send, recv, d):
        return pltpu.make_async_remote_copy(
            src_ref=src, dst_ref=dst, send_sem=send.at[d - 1], recv_sem=recv.at[d - 1],
            device_id=(me_s, lax.rem(me_t + d, nt)), device_id_type=MESH,
        )

    def to_pair(src, dst, send, recv, e):
        return pltpu.make_async_remote_copy(
            src_ref=src, dst_ref=dst, send_sem=send.at[e - 1], recv_sem=recv.at[e - 1],
            device_id=(me_s if e < nt else mate, lax.rem(me_t + e % nt, nt)),
            device_id_type=MESH,
        )

    def to_seq(src, dst, send, recv, d, target):
        return pltpu.make_async_remote_copy(
            src_ref=src, dst_ref=dst, send_sem=send.at[d - 1], recv_sem=recv.at[d - 1],
            device_id=(target, me_t), device_id_type=MESH,
        )

    pl.semaphore_wait(barrier, nt - 1 + ns - 1 + nt - 1)
    x_copies = [to_tp(tok, xg.at[me_t], x_send, x_recv, d) for d in range(1, nt)]
    for copy in x_copies:
        copy.start()

    first[2].wait()
    row = iota((rows, 1), 0)
    req = row % reqs
    base = jnp.where(req == 0, seen[0], 0)
    for r in range(1, reqs):
        base = jnp.where(req == r, slen[r - 1], base)
    position = (base + row // reqs).astype(F32)
    sine, cosine = sine_cosine(position * fr_v[...])
    front = iota((rows, ql), 1) % HD < HALF
    signed_sine = jnp.where(front, -sine, sine)
    q_rows, k_rows, m_rows = rows * heads, rows * kvl, reqs * heads
    i = iota((q_rows, 1), 0)
    order_q = one_hot(
        iota((q_rows, q_rows), 1)
        == (i % heads) * rows + (i // heads % steps) * reqs + i // (heads * steps)
    )
    i = iota((k_rows, 1), 0)
    order_k = one_hot(
        iota((k_rows, k_rows), 1)
        == (i // steps % kvl) * rows + (i % steps) * reqs + i // (steps * kvl)
    )
    lane128 = iota((128, 128), 0)
    spread_top = one_hot((lane128 >= HD) & (lane128 < HD + 3))
    spread_heads = one_hot(iota((HD, ql), 1) % HD == iota((HD, ql), 0))
    own_head = iota((m_rows, ql), 1) // HD == iota((m_rows, ql), 0) % heads
    join_heads = one_hot(iota((8, m_rows), 1) // heads == iota((8, m_rows), 0))

    for n, copy in enumerate(first + cached):
        if n != 2:
            copy.wait()
    for copy in later:
        copy.start()
    for copy in x_copies:
        copy.wait()
    pieces = [xg[c].astype(F32).reshape(rows, dl) for c in range(nt)]
    square = jnp.zeros((rows, 1), F32)
    for piece in pieces:
        square = square + jnp.sum(piece * piece, axis=-1, keepdims=True)
    inverse = lax.rsqrt(square * np.float32(1.0 / model) + EPS)
    gain = ag_v[...].astype(F32)[None]
    normed = [
        (piece * inverse * gain[:, c * dl : (c + 1) * dl]).astype(BF16)
        for c, piece in enumerate(pieces)
    ]

    def project(parts, weight):
        total = None
        for c, part in enumerate(parts):
            term = dot(part, weight[c * dl : (c + 1) * dl, :])
            total = term if total is None else total + term
        return total

    def project_t(parts, weight):
        total = None
        for c, part in enumerate(parts):
            term = dot_t(part, weight[:, c * dl : (c + 1) * dl])
            total = term if total is None else total + term
        return total

    def stack(v, count):
        return jnp.concatenate([v[:, k * HD : (k + 1) * HD] for k in range(count)], axis=0)

    key = rope(project_t(normed, wk_v), cosine[:, :kl], signed_sine[:, :kl], front[:, :kl])
    value = project_t(normed, wv_v)
    query = rope(project(normed, wq_v), cosine, signed_sine, front)
    key = dot(order_k, stack(key, kvl).astype(BF16))
    value = dot(order_k, stack(value, kvl).astype(BF16))
    query = dot(order_q, stack(query, heads).astype(BF16))

    short_k = sk_v[...].reshape(short_slots * kvl, sk.shape[2])
    short_v = sv_v[...].reshape(short_slots * kvl, sv.shape[2])
    row_count = heads * steps
    new_count = kvl * steps
    i = iota((row_count, 1), 0)
    step_of = i // heads
    kv_of = i % heads // GROUP
    new_col = iota((1, new_count), 1)
    new_mask = (kv_of == new_col // steps) & (new_col % steps <= step_of) & (me_s == 0)
    lane = iota((row_count, 128), 1)

    def by_kv(terms):
        total = terms[0]
        for k in range(1, kvl):
            total = jnp.where(kv_of == k, terms[k], total)
        return total

    blocks = []
    for r in range(reqs):
        q_r = query[r * row_count : (r + 1) * row_count].astype(BF16)
        k_r = key[r * new_count : (r + 1) * new_count].astype(BF16)
        v_r = value[r * new_count : (r + 1) * new_count].astype(BF16)
        if r == 0:
            slot = me_s * long_slots + iota((1, long_slots), 1)
            old_mask = ((slot - seen[0]) & (WIN - 1)) > step_of
            old_dots = by_kv([dot(q_r, lk_v[k]) for k in range(kvl)])
        else:
            cut = slice((r - 1) * HD, r * HD)
            col = iota((1, short_slots * kvl), 1)
            slot = me_s * short_slots + col // kvl
            old_mask = (kv_of == col % kvl) & (slot < slen[r - 1])
            old_dots = dot_t(q_r, short_k[:, cut])
        old_score = jnp.where(old_mask, old_dots * SCALE, HIDDEN_SCORE)
        new_score = jnp.where(new_mask, dot_t(q_r, k_r) * SCALE, HIDDEN_SCORE)
        top = jnp.maximum(
            jnp.max(old_score, axis=-1, keepdims=True), jnp.max(new_score, axis=-1, keepdims=True)
        )
        old_w = jnp.where(old_mask, jnp.exp(old_score - top), 0.0)
        new_w = jnp.where(new_mask, jnp.exp(new_score - top), 0.0)
        total = jnp.sum(old_w, axis=-1, keepdims=True) + jnp.sum(new_w, axis=-1, keepdims=True)
        old_w = old_w.astype(BF16)
        if r == 0:
            acc = by_kv([dot_t(old_w, lv_v[k]) for k in range(kvl)])
        else:
            acc = dot(old_w, short_v[:, cut])
        acc = acc + dot(new_w.astype(BF16), v_r)
        full = jnp.concatenate([acc, jnp.zeros((row_count, 128 - HD), F32)], axis=1)
        terms = []
        for number, count in ((top, 3), (total, 2)):
            rest = number
            for _ in range(count):
                term = rest.astype(BF16).astype(F32)
                terms.append(term)
                rest = rest - term
        for n, term in enumerate(terms):
            full = jnp.where(lane == HD + n, term, full)
        blocks.append(full)
    for t in range(steps):
        sb[t] = jnp.concatenate(
            [full[t * heads : (t + 1) * heads] for full in blocks], axis=0
        ).astype(BF16)

    s_copies = []
    for d in range(1, ns):
        target = lax.rem(me_s + d, ns)
        s_copies.append(
            to_seq(sb.at[target // copies_of_step], rb.at[d - 1], s_send, s_recv, d, target)
        )
    for copy in s_copies:
        copy.start()
    stream = [xg[c, my_step].astype(F32) for c in range(nt)]
    mate_stream = [xg[c, mate_step].astype(F32) for c in range(nt)]
    for copy in s_copies:
        copy.wait()
    parts = [sb[my_step]] + [rb[d] for d in range(ns - 1)]
    tops = [dot(part, spread_top) for part in parts]
    top = functools.reduce(jnp.maximum, tops)
    merged = jnp.zeros((m_rows, 128), F32)
    for part, part_top in zip(parts, tops):
        merged = merged + part.astype(F32) * jnp.exp(part_top - top)
    attended = merged[:, :HD] / (merged[:, HD + 3 : HD + 4] + merged[:, HD + 4 : HD + 5])
    attended = jnp.where(own_head, dot(attended.astype(BF16), spread_heads), 0.0).astype(BF16)
    attended = dot(join_heads, attended).astype(BF16)

    later[1].wait()
    head_term = dot(attended, wo_v[...])[:reqs]
    head_parts = [head_term[:, c * dl : (c + 1) * dl] for c in range(nt)]
    ob[...] = jnp.concatenate(head_parts, axis=0).astype(BF16)
    o_copies = [to_pair(ob, orb.at[e - 1], o_send, o_recv, e) for e in range(1, 2 * nt)]
    for copy in o_copies:
        copy.start()
    stream = [a + b for a, b in zip(stream, head_parts)]
    later[0].wait()
    gain = mg_v[...].astype(F32)[None]
    for copy in o_copies:
        copy.wait()

    def summed(slots):
        got = orb[slots[0]].astype(F32)
        for slot in slots[1:]:
            got = got + orb[slot].astype(F32)
        return [got[c * reqs : (c + 1) * reqs] for c in range(nt)]

    stream = [a + b for a, b in zip(stream, summed(range(nt - 1)))]
    mate_stream = [a + b for a, b in zip(mate_stream, summed(range(nt - 1, 2 * nt - 1)))]
    both = [jnp.concatenate([a, b], axis=0) for a, b in zip(stream, mate_stream)]
    square = jnp.zeros((2 * reqs, 1), F32)
    for piece in both:
        square = square + jnp.sum(piece * piece, axis=-1, keepdims=True)
    inverse = lax.rsqrt(square * np.float32(1.0 / model) + EPS)
    mlp_in = [
        (piece * inverse * gain[:, c * dl : (c + 1) * dl]).astype(BF16)
        for c, piece in enumerate(both)
    ]
    later[2].wait()
    gate = project_t(mlp_in, wg_v)
    later[3].wait()
    lift = project_t(mlp_in, wu_v)
    hidden = gate / (1.0 + jnp.exp(-gate)) * lift
    if 2 * share > ff:
        shared = (iota((1, share), 1) < 2 * share - ff) & (half == 1)
        hidden = jnp.where(shared, 0.0, hidden)
    later[4].wait()
    down = dot(hidden.astype(BF16), wd_v[...])
    result = jnp.zeros((reqs, dl), F32)
    for c in range(nt):
        piece = down[:, c * dl : (c + 1) * dl]
        db[0, c] = piece[:reqs].astype(BF16)
        db[1, c] = piece[reqs:].astype(BF16)
        result = result + jnp.where(me_t == c, stream[c] + piece[:reqs], 0.0)
    d_copies = [
        to_pair(
            db.at[e // nt, lax.rem(me_t + e % nt, nt)], drb.at[e - 1], d_send, d_recv, e
        )
        for e in range(1, 2 * nt)
    ]
    for copy in d_copies:
        copy.start()
    for copy in d_copies:
        copy.wait()
    for e in range(2 * nt - 1):
        result = result + drb[e].astype(F32)
    fb[...] = result.astype(BF16)

    f_copies = []
    for d in range(1, steps):
        target = lax.rem(my_step + d, steps) * copies_of_step + my_twin
        f_copies.append(to_seq(fb, out.at[my_step], f_send, f_recv, d, target))
    for copy in f_copies:
        copy.start()
    own = pltpu.make_async_copy(fb, out.at[my_step], local_sem.at[14 + nt])
    own.start()
    for copy in f_copies:
        copy.wait()
    own.wait()


def body(
    ns, nt, tokens_in, attn_gain, mlp_gain, proj_query, proj_key, proj_value, proj_out,
    proj_gate, proj_up, proj_down, long_keys, long_values, short_keys, short_values,
    long_seen, short_len,
):
    steps, reqs, dl = tokens_in.shape
    ql = proj_query.shape[1]
    rows = steps * reqs
    m_rows = reqs * (ql // HD)
    index = (np.arange(ql) % HD) % HALF
    freq = (THETA ** (-2.0 * index.astype(np.float64) / HD)).astype(np.float32)[None]
    operands = (
        tokens_in, attn_gain, mlp_gain, proj_query, proj_key.T, proj_value.T,
        proj_out, proj_gate.T, proj_up.T, proj_down, long_keys.transpose(1, 2, 0),
        long_values.transpose(1, 2, 0), short_keys, short_values, jnp.asarray(freq),
    )
    ff = proj_down.shape[0]
    share = -(-ff // 32) * 16
    dma = pltpu.SemaphoreType.DMA
    return pl.pallas_call(
        functools.partial(kernel, ns, nt),
        out_shape=jax.ShapeDtypeStruct(tokens_in.shape, BF16),
        in_specs=[pl.BlockSpec(memory_space=pl.ANY)] * len(operands)
        + [pl.BlockSpec(memory_space=pltpu.SMEM)] * 2,
        out_specs=pl.BlockSpec(memory_space=pl.ANY),
        scratch_shapes=[
            pltpu.VMEM((share if a.shape[0] == ff else a.shape[0],) + a.shape[1:], a.dtype)
            for a in operands[1:]
        ]
        + [
            pltpu.VMEM((nt, steps, reqs, dl), BF16),
            pltpu.VMEM((steps, m_rows, 128), BF16),
            pltpu.VMEM((ns - 1, m_rows, 128), BF16),
            pltpu.VMEM((nt * reqs, dl), BF16),
            pltpu.VMEM((2 * nt - 1, nt * reqs, dl), BF16),
            pltpu.VMEM((2, nt, reqs, dl), BF16),
            pltpu.VMEM((2 * nt - 1, reqs, dl), BF16),
            pltpu.VMEM((reqs, dl), BF16),
            dma((15 + nt,)),
            dma((nt - 1,)), dma((nt - 1,)),
            dma((ns - 1,)), dma((ns - 1,)),
            dma((2 * nt - 1,)), dma((2 * nt - 1,)),
            dma((2 * nt - 1,)), dma((2 * nt - 1,)),
            dma((steps - 1,)), dma((steps - 1,)),
        ],
        compiler_params=pltpu.CompilerParams(
            collective_id=0, has_side_effects=True, vmem_limit_bytes=60 * 1024 * 1024
        ),
    )(*operands, long_seen, short_len)


def solution(mesh):
    ns, nt = mesh.shape["seq"], mesh.shape["tp"]
    in_specs = (
        P(None, None, "tp"),
        P(),
        P(),
        P(None, "tp"),
        P(None, "tp"),
        P(None, "tp"),
        P("tp", None),
        P(None, "tp"),
        P(None, "tp"),
        P("tp", None),
        P("seq", "tp", None),
        P("seq", "tp", None),
        P("seq", "tp", None),
        P("seq", "tp", None),
        P(),
        P(),
    )
    return jax.shard_map(
        functools.partial(body, ns, nt),
        mesh=mesh,
        in_specs=in_specs,
        out_specs=P(None, None, "tp"),
        check_vma=False,
    )
```

```python
import functools
import math

import jax
import jax.numpy as jnp
import numpy as np
from jax import lax
from jax.experimental import pallas as pl
from jax.experimental.pallas import tpu as pltpu
from jax.sharding import PartitionSpec as P

HEADS = 32
KV_HEADS = 8
HD = 80
HALF = HD // 2
GROUP = HEADS // KV_HEADS
WIN = 4096
STEPS = 8

EPS = 1e-05
THETA = 10000.0
HIDDEN_SCORE = -1e30
SCALE = 1.0 / math.sqrt(HD)
F32 = jnp.float32
BF16 = jnp.bfloat16
MESH = pl.DeviceIdType.MESH


def dot(a, b):
    return lax.dot_general(a, b, (((1,), (0,)), ((), ())), preferred_element_type=F32)


def dot_t(a, b):
    return lax.dot_general(a, b, (((1,), (1,)), ((), ())), preferred_element_type=F32)


def pad_rows(v, rows):
    if v.shape[0] == rows:
        return v
    return jnp.concatenate([v, jnp.zeros((rows - v.shape[0], v.shape[1]), v.dtype)], axis=0)


def iota(shape, axis):
    return lax.broadcasted_iota(jnp.int32, shape, axis)


def flip(index, mask):
    bit = 1
    while bit <= mask:
        if mask & bit:
            index = index + bit - 2 * bit * (index // bit % 2)
        bit *= 2
    return index


def one_hot(condition):
    return jnp.where(condition, 1.0, 0.0).astype(BF16)


def sine_cosine(angle):
    turns = jnp.floor(angle * np.float32(2.0 / math.pi) + 0.5)
    rest = angle - turns * np.float32(1.5703125)
    rest = rest - turns * np.float32(4.8351287841796875e-4)
    rest = rest - turns * np.float32(math.pi / 2 - 1.5703125 - 4.8351287841796875e-4)
    sq = rest * rest
    sine = rest + rest * sq * (
        np.float32(-1.6666654611e-1)
        + sq * (np.float32(8.3321608736e-3) + sq * np.float32(-1.9515295891e-4))
    )
    cosine = 1.0 - 0.5 * sq + sq * sq * (
        np.float32(4.166664568298827e-2)
        + sq * (np.float32(-1.388731625493765e-3) + sq * np.float32(2.443315711809948e-5))
    )
    quarter = turns - 4.0 * jnp.floor(turns * 0.25)
    odd = (quarter == 1.0) | (quarter == 3.0)
    sin_out = jnp.where(odd, cosine, sine)
    cos_out = jnp.where(odd, sine, cosine)
    sin_out = jnp.where(quarter >= 2.0, -sin_out, sin_out)
    cos_out = jnp.where((quarter == 1.0) | (quarter == 2.0), -cos_out, cos_out)
    return sin_out, cos_out


def rope(v, cosine, signed_sine, front):
    ahead = jnp.concatenate([v[:, HALF:], v[:, :HALF]], axis=1)
    behind = jnp.concatenate([v[:, -HALF:], v[:, :-HALF]], axis=1)
    return v * cosine + jnp.where(front, ahead, behind) * signed_sine


def kernel(
    ns, nt, tok, ag, mg, wq, wk, wv, wo, wg, wu, wd, lk, lv, sk, sv, fr, seen, slen, out,
    ag_v, mg_v, wq_v, wk_v, wv_v, wo_v, wg_v, wu_v, wd_v, lk_v, lv_v, sk_v, sv_v, fr_v,
    xg, sb, rb, ob, orb, db, drb, fb, local_sem,
    x_send, x_recv, s_send, s_recv, o_send, o_recv, d_send, d_recv, f_send, f_recv,
):
    me_s = lax.axis_index("seq")
    me_t = lax.axis_index("tp")
    steps, reqs, dl = tok.shape
    rows = steps * reqs
    copies_of_step = ns // steps
    my_step = me_s // copies_of_step
    my_twin = lax.rem(me_s, copies_of_step)
    half = lax.rem(my_step, 2)
    mate_step = my_step + 1 - 2 * half
    mate = mate_step * copies_of_step + my_twin
    ff, share = wd.shape[0], wd_v.shape[0]
    low = pl.multiple_of(half * (ff - share), 16)
    model = wq.shape[0]
    ql = wq.shape[1]
    kl = wk.shape[0]
    heads = ql // HD
    kvl = kl // HD
    long_slots = lk.shape[2]
    short_slots = sk.shape[0]

    barrier = pltpu.get_barrier_semaphore()
    for d in range(1, nt):
        pl.semaphore_signal(
            barrier, inc=1, device_id=(me_s, lax.rem(me_t + d, nt)), device_id_type=MESH
        )
    for d in range(1, ns):
        pl.semaphore_signal(
            barrier, inc=1, device_id=(lax.rem(me_s + d, ns), me_t), device_id_type=MESH
        )

    for d in range(1, nt):
        pl.semaphore_signal(
            barrier, inc=1, device_id=(mate, lax.rem(me_t + d, nt)), device_id_type=MESH
        )

    def load(n, src, dst):
        return pltpu.make_async_copy(src, dst, local_sem.at[n])

    first = [
        load(0, wk, wk_v), load(1, wv, wv_v), load(2, fr, fr_v), load(3, ag, ag_v),
        load(4, tok, xg.at[me_t]),
    ]
    first += [
        load(5 + c, wq.at[pl.ds(c * dl, dl)], wq_v.at[pl.ds(c * dl, dl)]) for c in range(nt)
    ]
    cached = [
        load(5 + nt + n, src, dst)
        for n, (src, dst) in enumerate([(lk, lk_v), (sk, sk_v), (lv, lv_v), (sv, sv_v)])
    ]
    later = [
        load(9 + nt + n, src, dst)
        for n, (src, dst) in enumerate(
            [
                (mg, mg_v),
                (wo, wo_v),
                (wg.at[pl.ds(low, share)], wg_v),
                (wu.at[pl.ds(low, share)], wu_v),
                (wd.at[pl.ds(low, share)], wd_v),
            ]
        )
    ]
    for copy in first + cached:
        copy.start()

    def to_pair(src, dst, send, recv, e):
        return pltpu.make_async_remote_copy(
            src_ref=src, dst_ref=dst, send_sem=send.at[e - 1], recv_sem=recv.at[e - 1],
            device_id=(me_s if e < nt else mate, lax.rem(me_t + e % nt, nt)),
            device_id_type=MESH,
        )

    def to_seq(src, dst, send, recv, d, target):
        return pltpu.make_async_remote_copy(
            src_ref=src, dst_ref=dst, send_sem=send.at[d - 1], recv_sem=recv.at[d - 1],
            device_id=(target, me_t), device_id_type=MESH,
        )

    pl.semaphore_wait(barrier, nt - 1 + ns - 1 + nt - 1)
    x_copies = [
        pltpu.make_async_remote_copy(
            src_ref=tok, dst_ref=xg.at[me_t], send_sem=x_send.at[d - 1],
            recv_sem=x_recv.at[d - 1], device_id=(me_s, flip(me_t, d)), device_id_type=MESH,
        )
        for d in range(1, nt)
    ]
    for copy in x_copies:
        copy.start()

    first[2].wait()
    row = iota((rows, 1), 0)
    req = row % reqs
    base = jnp.where(req == 0, seen[0], 0)
    for r in range(1, reqs):
        base = jnp.where(req == r, slen[r - 1], base)
    position = (base + row // reqs).astype(F32)
    sine, cosine = sine_cosine(position * fr_v[...])
    front = iota((rows, ql), 1) % HD < HALF
    signed_sine = jnp.where(front, -sine, sine)
    q_rows, k_rows, m_rows = rows * heads, rows * kvl, reqs * heads
    i = iota((q_rows, 1), 0)
    order_q = one_hot(
        iota((q_rows, q_rows), 1)
        == (i % heads) * rows + (i // heads % steps) * reqs + i // (heads * steps)
    )
    i = iota((k_rows, 1), 0)
    order_k = one_hot(
        iota((k_rows, k_rows), 1)
        == (i // steps % kvl) * rows + (i % steps) * reqs + i // (steps * kvl)
    )
    lane128 = iota((128, 128), 0)
    spread_top = one_hot((lane128 >= HD) & (lane128 < HD + 3))
    spread_heads = one_hot(iota((HD, ql), 1) % HD == iota((HD, ql), 0))
    own_head = iota((m_rows, ql), 1) // HD == iota((m_rows, ql), 0) % heads
    join_heads = one_hot(iota((8, m_rows), 1) // heads == iota((8, m_rows), 0))

    for n, copy in enumerate(first + cached):
        if n != 2:
            copy.wait()
    for copy in later:
        copy.start()
    gain = ag_v[...].astype(F32)[None]
    gains = [gain[:, c * dl : (c + 1) * dl] for c in range(nt)]
    square = jnp.zeros((rows, 1), F32)
    query = jnp.zeros((rows, ql), F32)
    key = jnp.zeros((rows, kl), F32)
    value = jnp.zeros((rows, kl), F32)
    in_turn = dl % 128 == 0
    if not in_turn:
        for copy in x_copies:
            copy.wait()
    for d in range(nt):
        if in_turn:
            if d:
                x_copies[d - 1].wait()
            c = flip(me_t, d)
            here = pl.ds(pl.multiple_of(c * dl, 128), dl)
            gain = gains[0]
            for n in range(1, nt):
                gain = jnp.where(c == n, gains[n], gain)
        else:
            c, here, gain = d, pl.ds(d * dl, dl), gains[d]
        piece = xg[c].astype(F32).reshape(rows, dl)
        square = square + jnp.sum(piece * piece, axis=-1, keepdims=True)
        piece = (piece * gain).astype(BF16)
        key = key + dot_t(piece, wk_v[:, here])
        value = value + dot_t(piece, wv_v[:, here])
        query = query + dot(piece, wq_v[here, :])
    inverse = lax.rsqrt(square * np.float32(1.0 / model) + EPS)

    def project_t(parts, weight):
        total = None
        for c, part in enumerate(parts):
            term = dot_t(part, weight[:, c * dl : (c + 1) * dl])
            total = term if total is None else total + term
        return total

    def stack(v, count):
        return jnp.concatenate([v[:, k * HD : (k + 1) * HD] for k in range(count)], axis=0)

    key = rope(key * inverse, cosine[:, :kl], signed_sine[:, :kl], front[:, :kl])
    value = value * inverse
    query = rope(query * inverse, cosine, signed_sine, front)
    key = dot(order_k, stack(key, kvl).astype(BF16))
    value = dot(order_k, stack(value, kvl).astype(BF16))
    query = dot(order_q, stack(query, heads).astype(BF16))

    short_k = sk_v[...].reshape(short_slots * kvl, sk.shape[2])
    short_v = sv_v[...].reshape(short_slots * kvl, sv.shape[2])
    row_count = heads * steps
    new_count = kvl * steps
    i = iota((row_count, 1), 0)
    step_of = i // heads
    kv_of = i % heads // GROUP
    new_col = iota((1, new_count), 1)
    new_mask = (kv_of == new_col // steps) & (new_col % steps <= step_of) & (me_s == 0)
    lane = iota((row_count, 128), 1)

    def by_kv(terms):
        total = terms[0]
        for k in range(1, kvl):
            total = jnp.where(kv_of == k, terms[k], total)
        return total

    blocks = []
    for r in range(reqs):
        q_r = query[r * row_count : (r + 1) * row_count].astype(BF16)
        k_r = key[r * new_count : (r + 1) * new_count].astype(BF16)
        v_r = value[r * new_count : (r + 1) * new_count].astype(BF16)
        if r == 0:
            slot = me_s * long_slots + iota((1, long_slots), 1)
            old_mask = ((slot - seen[0]) & (WIN - 1)) > step_of
            old_dots = by_kv([dot(q_r, lk_v[k]) for k in range(kvl)])
        else:
            cut = slice((r - 1) * HD, r * HD)
            col = iota((1, short_slots * kvl), 1)
            slot = me_s * short_slots + col // kvl
            old_mask = (kv_of == col % kvl) & (slot < slen[r - 1])
            old_dots = dot_t(q_r, short_k[:, cut])
        old_score = jnp.where(old_mask, old_dots * SCALE, HIDDEN_SCORE)
        new_score = jnp.where(new_mask, dot_t(q_r, k_r) * SCALE, HIDDEN_SCORE)
        top = jnp.maximum(
            jnp.max(old_score, axis=-1, keepdims=True), jnp.max(new_score, axis=-1, keepdims=True)
        )
        old_w = jnp.where(old_mask, jnp.exp(old_score - top), 0.0)
        new_w = jnp.where(new_mask, jnp.exp(new_score - top), 0.0)
        total = jnp.sum(old_w, axis=-1, keepdims=True) + jnp.sum(new_w, axis=-1, keepdims=True)
        old_w = old_w.astype(BF16)
        if r == 0:
            acc = by_kv([dot_t(old_w, lv_v[k]) for k in range(kvl)])
        else:
            acc = dot(old_w, short_v[:, cut])
        acc = acc + dot(new_w.astype(BF16), v_r)
        full = jnp.concatenate([acc, jnp.zeros((row_count, 128 - HD), F32)], axis=1)
        terms = []
        for number, count in ((top, 3), (total, 2)):
            rest = number
            for _ in range(count):
                term = rest.astype(BF16).astype(F32)
                terms.append(term)
                rest = rest - term
        for n, term in enumerate(terms):
            full = jnp.where(lane == HD + n, term, full)
        blocks.append(full)
    for t in range(steps):
        sb[t] = jnp.concatenate(
            [full[t * heads : (t + 1) * heads] for full in blocks], axis=0
        ).astype(BF16)

    s_copies = []
    for d in range(1, ns):
        target = lax.rem(me_s + d, ns)
        s_copies.append(
            to_seq(sb.at[target // copies_of_step], rb.at[d - 1], s_send, s_recv, d, target)
        )
    for copy in s_copies:
        copy.start()
    stream = [xg[c, my_step].astype(F32) for c in range(nt)]
    mate_stream = [xg[c, mate_step].astype(F32) for c in range(nt)]
    for copy in s_copies:
        copy.wait()
    parts = [sb[my_step]] + [rb[d] for d in range(ns - 1)]
    tops = [dot(part, spread_top) for part in parts]
    top = functools.reduce(jnp.maximum, tops)
    merged = jnp.zeros((m_rows, 128), F32)
    for part, part_top in zip(parts, tops):
        merged = merged + part.astype(F32) * jnp.exp(part_top - top)
    attended = merged[:, :HD] / (merged[:, HD + 3 : HD + 4] + merged[:, HD + 4 : HD + 5])
    attended = jnp.where(own_head, dot(attended.astype(BF16), spread_heads), 0.0).astype(BF16)
    attended = dot(join_heads, attended).astype(BF16)

    later[1].wait()
    head_term = dot(attended, wo_v[...])[:reqs]
    head_parts = [head_term[:, c * dl : (c + 1) * dl] for c in range(nt)]
    ob[...] = jnp.concatenate(head_parts, axis=0).astype(BF16)
    o_copies = [to_pair(ob, orb.at[e - 1], o_send, o_recv, e) for e in range(1, 2 * nt)]
    for copy in o_copies:
        copy.start()
    stream = [a + b for a, b in zip(stream, head_parts)]
    later[0].wait()
    gain = mg_v[...].astype(F32)[None]
    for copy in o_copies:
        copy.wait()

    def summed(slots):
        got = orb[slots[0]].astype(F32)
        for slot in slots[1:]:
            got = got + orb[slot].astype(F32)
        return [got[c * reqs : (c + 1) * reqs] for c in range(nt)]

    stream = [a + b for a, b in zip(stream, summed(range(nt - 1)))]
    mate_stream = [a + b for a, b in zip(mate_stream, summed(range(nt - 1, 2 * nt - 1)))]
    both = [jnp.concatenate([a, b], axis=0) for a, b in zip(stream, mate_stream)]
    square = jnp.zeros((2 * reqs, 1), F32)
    for piece in both:
        square = square + jnp.sum(piece * piece, axis=-1, keepdims=True)
    inverse = lax.rsqrt(square * np.float32(1.0 / model) + EPS)
    mlp_in = [
        (piece * inverse * gain[:, c * dl : (c + 1) * dl]).astype(BF16)
        for c, piece in enumerate(both)
    ]
    later[2].wait()
    gate = project_t(mlp_in, wg_v)
    later[3].wait()
    lift = project_t(mlp_in, wu_v)
    hidden = gate / (1.0 + jnp.exp(-gate)) * lift
    if 2 * share > ff:
        shared = (iota((1, share), 1) < 2 * share - ff) & (half == 1)
        hidden = jnp.where(shared, 0.0, hidden)
    later[4].wait()
    down = dot(hidden.astype(BF16), wd_v[...])
    result = jnp.zeros((reqs, dl), F32)
    for c in range(nt):
        piece = down[:, c * dl : (c + 1) * dl]
        db[0, c] = piece[:reqs].astype(BF16)
        db[1, c] = piece[reqs:].astype(BF16)
        result = result + jnp.where(me_t == c, stream[c] + piece[:reqs], 0.0)
    d_copies = [
        to_pair(
            db.at[e // nt, lax.rem(me_t + e % nt, nt)], drb.at[e - 1], d_send, d_recv, e
        )
        for e in range(1, 2 * nt)
    ]
    for copy in d_copies:
        copy.start()
    for copy in d_copies:
        copy.wait()
    for e in range(2 * nt - 1):
        result = result + drb[e].astype(F32)
    fb[...] = result.astype(BF16)

    f_copies = []
    for d in range(1, steps):
        target = lax.rem(my_step + d, steps) * copies_of_step + my_twin
        f_copies.append(to_seq(fb, out.at[my_step], f_send, f_recv, d, target))
    for copy in f_copies:
        copy.start()
    own = pltpu.make_async_copy(fb, out.at[my_step], local_sem.at[14 + nt])
    own.start()
    for copy in f_copies:
        copy.wait()
    own.wait()


def body(
    ns, nt, tokens_in, attn_gain, mlp_gain, proj_query, proj_key, proj_value, proj_out,
    proj_gate, proj_up, proj_down, long_keys, long_values, short_keys, short_values,
    long_seen, short_len,
):
    steps, reqs, dl = tokens_in.shape
    ql = proj_query.shape[1]
    rows = steps * reqs
    m_rows = reqs * (ql // HD)
    index = (np.arange(ql) % HD) % HALF
    freq = (THETA ** (-2.0 * index.astype(np.float64) / HD)).astype(np.float32)[None]
    operands = (
        tokens_in, attn_gain, mlp_gain, proj_query, proj_key.T, proj_value.T,
        proj_out, proj_gate.T, proj_up.T, proj_down, long_keys.transpose(1, 2, 0),
        long_values.transpose(1, 2, 0), short_keys, short_values, jnp.asarray(freq),
    )
    ff = proj_down.shape[0]
    share = -(-ff // 32) * 16
    dma = pltpu.SemaphoreType.DMA
    return pl.pallas_call(
        functools.partial(kernel, ns, nt),
        out_shape=jax.ShapeDtypeStruct(tokens_in.shape, BF16),
        in_specs=[pl.BlockSpec(memory_space=pl.ANY)] * len(operands)
        + [pl.BlockSpec(memory_space=pltpu.SMEM)] * 2,
        out_specs=pl.BlockSpec(memory_space=pl.ANY),
        scratch_shapes=[
            pltpu.VMEM((share if a.shape[0] == ff else a.shape[0],) + a.shape[1:], a.dtype)
            for a in operands[1:]
        ]
        + [
            pltpu.VMEM((nt, steps, reqs, dl), BF16),
            pltpu.VMEM((steps, m_rows, 128), BF16),
            pltpu.VMEM((ns - 1, m_rows, 128), BF16),
            pltpu.VMEM((nt * reqs, dl), BF16),
            pltpu.VMEM((2 * nt - 1, nt * reqs, dl), BF16),
            pltpu.VMEM((2, nt, reqs, dl), BF16),
            pltpu.VMEM((2 * nt - 1, reqs, dl), BF16),
            pltpu.VMEM((reqs, dl), BF16),
            dma((15 + nt,)),
            dma((nt - 1,)), dma((nt - 1,)),
            dma((ns - 1,)), dma((ns - 1,)),
            dma((2 * nt - 1,)), dma((2 * nt - 1,)),
            dma((2 * nt - 1,)), dma((2 * nt - 1,)),
            dma((steps - 1,)), dma((steps - 1,)),
        ],
        compiler_params=pltpu.CompilerParams(
            collective_id=0, has_side_effects=True, vmem_limit_bytes=60 * 1024 * 1024
        ),
    )(*operands, long_seen, short_len)


def solution(mesh):
    ns, nt = mesh.shape["seq"], mesh.shape["tp"]
    in_specs = (
        P(None, None, "tp"),
        P(),
        P(),
        P(None, "tp"),
        P(None, "tp"),
        P(None, "tp"),
        P("tp", None),
        P(None, "tp"),
        P(None, "tp"),
        P("tp", None),
        P("seq", "tp", None),
        P("seq", "tp", None),
        P("seq", "tp", None),
        P("seq", "tp", None),
        P(),
        P(),
    )
    return jax.shard_map(
        functools.partial(body, ns, nt),
        mesh=mesh,
        in_specs=in_specs,
        out_specs=P(None, None, "tp"),
        check_vma=False,
    )
```

```python
import functools
import math

import jax
import jax.numpy as jnp
import numpy as np
from jax import lax
from jax.experimental import pallas as pl
from jax.experimental.pallas import tpu as pltpu
from jax.sharding import PartitionSpec as P

HEADS = 32
KV_HEADS = 8
HD = 80
HALF = HD // 2
GROUP = HEADS // KV_HEADS
WIN = 4096
STEPS = 8

EPS = 1e-05
THETA = 10000.0
HIDDEN_SCORE = -1e30
SCALE = 1.0 / math.sqrt(HD)
F32 = jnp.float32
BF16 = jnp.bfloat16
MESH = pl.DeviceIdType.MESH


def dot(a, b):
    return lax.dot_general(a, b, (((1,), (0,)), ((), ())), preferred_element_type=F32)


def dot_t(a, b):
    return lax.dot_general(a, b, (((1,), (1,)), ((), ())), preferred_element_type=F32)


def pad_rows(v, rows):
    if v.shape[0] == rows:
        return v
    return jnp.concatenate([v, jnp.zeros((rows - v.shape[0], v.shape[1]), v.dtype)], axis=0)


def iota(shape, axis):
    return lax.broadcasted_iota(jnp.int32, shape, axis)


def flip(index, mask):
    bit = 1
    while bit <= mask:
        if mask & bit:
            index = index + bit - 2 * bit * (index // bit % 2)
        bit *= 2
    return index


def one_hot(condition):
    return jnp.where(condition, 1.0, 0.0).astype(BF16)


def sine_cosine(angle):
    turns = jnp.floor(angle * np.float32(2.0 / math.pi) + 0.5)
    rest = angle - turns * np.float32(1.5703125)
    rest = rest - turns * np.float32(4.8351287841796875e-4)
    rest = rest - turns * np.float32(math.pi / 2 - 1.5703125 - 4.8351287841796875e-4)
    sq = rest * rest
    sine = rest + rest * sq * (
        np.float32(-1.6666654611e-1)
        + sq * (np.float32(8.3321608736e-3) + sq * np.float32(-1.9515295891e-4))
    )
    cosine = 1.0 - 0.5 * sq + sq * sq * (
        np.float32(4.166664568298827e-2)
        + sq * (np.float32(-1.388731625493765e-3) + sq * np.float32(2.443315711809948e-5))
    )
    quarter = turns - 4.0 * jnp.floor(turns * 0.25)
    odd = (quarter == 1.0) | (quarter == 3.0)
    sin_out = jnp.where(odd, cosine, sine)
    cos_out = jnp.where(odd, sine, cosine)
    sin_out = jnp.where(quarter >= 2.0, -sin_out, sin_out)
    cos_out = jnp.where((quarter == 1.0) | (quarter == 2.0), -cos_out, cos_out)
    return sin_out, cos_out


def rope(v, cosine, signed_sine, front):
    ahead = jnp.concatenate([v[:, HALF:], v[:, :HALF]], axis=1)
    behind = jnp.concatenate([v[:, -HALF:], v[:, :-HALF]], axis=1)
    return v * cosine + jnp.where(front, ahead, behind) * signed_sine


def kernel(
    ns, nt, tok, ag, mg, wq, wk, wv, wo, wg, wu, wd, lk, lv, sk, sv, fr, seen, slen, out,
    ag_v, mg_v, wq_v, wk_v, wv_v, wo_v, wg_v, wu_v, wd_v, lk_v, lv_v, sk_v, sv_v, fr_v,
    xg, sb, rb, ob, orb, db, drb, fb, local_sem,
    x_send, x_recv, s_send, s_recv, o_send, o_recv, d_send, d_recv, f_send, f_recv,
):
    me_s = lax.axis_index("seq")
    me_t = lax.axis_index("tp")
    steps, reqs, dl = tok.shape
    rows = steps * reqs
    copies_of_step = ns // steps
    my_step = me_s // copies_of_step
    my_twin = lax.rem(me_s, copies_of_step)
    half = lax.rem(my_step, 2)
    mate_step = my_step + 1 - 2 * half
    mate = mate_step * copies_of_step + my_twin
    ff, share = wd.shape[0], wd_v.shape[0]
    low = pl.multiple_of(half * (ff - share), 16)
    model = wq.shape[0]
    ql = wq.shape[1]
    kl = wk.shape[0]
    heads = ql // HD
    kvl = kl // HD
    long_slots = lk.shape[2]
    short_slots = sk.shape[0]

    barrier = pltpu.get_barrier_semaphore()
    for d in range(1, nt):
        pl.semaphore_signal(
            barrier, inc=1, device_id=(me_s, lax.rem(me_t + d, nt)), device_id_type=MESH
        )
    for d in range(1, ns):
        pl.semaphore_signal(
            barrier, inc=1, device_id=(lax.rem(me_s + d, ns), me_t), device_id_type=MESH
        )

    for d in range(1, nt):
        pl.semaphore_signal(
            barrier, inc=1, device_id=(mate, lax.rem(me_t + d, nt)), device_id_type=MESH
        )

    def load(n, src, dst):
        return pltpu.make_async_copy(src, dst, local_sem.at[n])

    first = [
        load(0, wk, wk_v), load(1, wv, wv_v), load(2, fr, fr_v), load(3, ag, ag_v),
        load(4, tok, xg.at[me_t]),
    ]
    first += [
        load(5 + c, wq.at[pl.ds(c * dl, dl)], wq_v.at[pl.ds(c * dl, dl)]) for c in range(nt)
    ]
    cached = [
        load(5 + nt + n, src, dst)
        for n, (src, dst) in enumerate([(lk, lk_v), (sk, sk_v), (lv, lv_v), (sv, sv_v)])
    ]
    later = [
        load(9 + nt + n, src, dst)
        for n, (src, dst) in enumerate(
            [
                (mg, mg_v),
                (wo, wo_v),
                (wg.at[pl.ds(low, share)], wg_v),
                (wu.at[pl.ds(low, share)], wu_v),
                (wd.at[pl.ds(low, share)], wd_v),
            ]
        )
    ]
    for copy in first + cached:
        copy.start()

    def to_pair(src, dst, send, recv, e):
        return pltpu.make_async_remote_copy(
            src_ref=src, dst_ref=dst, send_sem=send.at[e - 1], recv_sem=recv.at[e - 1],
            device_id=(me_s if e < nt else mate, lax.rem(me_t + e % nt, nt)),
            device_id_type=MESH,
        )

    def to_seq(src, dst, send, recv, d, target):
        return pltpu.make_async_remote_copy(
            src_ref=src, dst_ref=dst, send_sem=send.at[d - 1], recv_sem=recv.at[d - 1],
            device_id=(target, me_t), device_id_type=MESH,
        )

    pl.semaphore_wait(barrier, nt - 1 + ns - 1 + nt - 1)
    x_copies = [
        pltpu.make_async_remote_copy(
            src_ref=tok, dst_ref=xg.at[me_t], send_sem=x_send.at[d - 1],
            recv_sem=x_recv.at[d - 1], device_id=(me_s, flip(me_t, d)), device_id_type=MESH,
        )
        for d in range(1, nt)
    ]
    for copy in x_copies:
        copy.start()

    first[2].wait()
    row = iota((rows, 1), 0)
    req = row % reqs
    base = jnp.where(req == 0, seen[0], 0)
    for r in range(1, reqs):
        base = jnp.where(req == r, slen[r - 1], base)
    position = (base + row // reqs).astype(F32)
    sine, cosine = sine_cosine(position * fr_v[...])
    front = iota((rows, ql), 1) % HD < HALF
    signed_sine = jnp.where(front, -sine, sine)
    q_rows, k_rows, m_rows = rows * heads, rows * kvl, reqs * heads
    i = iota((q_rows, 1), 0)
    order_q = one_hot(
        iota((q_rows, q_rows), 1)
        == (i % heads) * rows + (i // heads % steps) * reqs + i // (heads * steps)
    )
    i = iota((k_rows, 1), 0)
    order_k = one_hot(
        iota((k_rows, k_rows), 1)
        == (i // steps % kvl) * rows + (i % steps) * reqs + i // (steps * kvl)
    )
    lane128 = iota((128, 128), 0)
    spread_top = one_hot((lane128 >= HD) & (lane128 < HD + 3))
    spread_heads = one_hot(iota((HD, ql), 1) % HD == iota((HD, ql), 0))
    own_head = iota((m_rows, ql), 1) // HD == iota((m_rows, ql), 0) % heads
    join_heads = one_hot(iota((8, m_rows), 1) // heads == iota((8, m_rows), 0))

    for n, copy in enumerate(first + cached):
        if n != 2:
            copy.wait()
    for copy in later:
        copy.start()
    short_k = sk_v[...].reshape(short_slots * kvl, sk.shape[2])
    short_v = sv_v[...].reshape(short_slots * kvl, sv.shape[2])
    row_count = heads * steps
    new_count = kvl * steps
    i = iota((row_count, 1), 0)
    step_of = i // heads
    kv_of = i % heads // GROUP
    new_col = iota((1, new_count), 1)
    new_mask = (kv_of == new_col // steps) & (new_col % steps <= step_of) & (me_s == 0)
    lane = iota((row_count, 128), 1)

    def by_kv(terms):
        total = terms[0]
        for k in range(1, kvl):
            total = jnp.where(kv_of == k, terms[k], total)
        return total

    short_keys = [short_k[:, r * HD : (r + 1) * HD] for r in range(reqs - 1)]
    short_values = [short_v[:, r * HD : (r + 1) * HD] for r in range(reqs - 1)]
    slot = me_s * long_slots + iota((1, long_slots), 1)
    old_masks = [((slot - seen[0]) & (WIN - 1)) > step_of]
    col = iota((1, short_slots * kvl), 1)
    slot = me_s * short_slots + col // kvl
    same_kv = kv_of == col % kvl
    old_masks += [same_kv & (slot < slen[r]) for r in range(reqs - 1)]

    gain = ag_v[...].astype(F32)[None]
    gains = [gain[:, c * dl : (c + 1) * dl] for c in range(nt)]
    square = jnp.zeros((rows, 1), F32)
    query = jnp.zeros((rows, ql), F32)
    key = jnp.zeros((rows, kl), F32)
    value = jnp.zeros((rows, kl), F32)
    in_turn = dl % 128 == 0
    if not in_turn:
        for copy in x_copies:
            copy.wait()
    for d in range(nt):
        if in_turn:
            if d:
                x_copies[d - 1].wait()
            c = flip(me_t, d)
            here = pl.ds(pl.multiple_of(c * dl, 128), dl)
            gain = gains[0]
            for n in range(1, nt):
                gain = jnp.where(c == n, gains[n], gain)
        else:
            c, here, gain = d, pl.ds(d * dl, dl), gains[d]
        piece = xg[c].astype(F32).reshape(rows, dl)
        square = square + jnp.sum(piece * piece, axis=-1, keepdims=True)
        piece = (piece * gain).astype(BF16)
        key = key + dot_t(piece, wk_v[:, here])
        value = value + dot_t(piece, wv_v[:, here])
        query = query + dot(piece, wq_v[here, :])
    inverse = lax.rsqrt(square * np.float32(1.0 / model) + EPS)

    def project_t(parts, weight):
        total = None
        for c, part in enumerate(parts):
            term = dot_t(part, weight[:, c * dl : (c + 1) * dl])
            total = term if total is None else total + term
        return total

    def stack(v, count):
        return jnp.concatenate([v[:, k * HD : (k + 1) * HD] for k in range(count)], axis=0)

    key = rope(key * inverse, cosine[:, :kl], signed_sine[:, :kl], front[:, :kl])
    value = value * inverse
    query = rope(query * inverse, cosine, signed_sine, front)
    key = dot(order_k, stack(key, kvl).astype(BF16))
    value = dot(order_k, stack(value, kvl).astype(BF16))
    query = dot(order_q, stack(query, heads).astype(BF16))

    blocks = []
    for r in range(reqs):
        q_r = query[r * row_count : (r + 1) * row_count].astype(BF16)
        k_r = key[r * new_count : (r + 1) * new_count].astype(BF16)
        v_r = value[r * new_count : (r + 1) * new_count].astype(BF16)
        old_mask = old_masks[r]
        if r == 0:
            old_dots = by_kv([dot(q_r, lk_v[k]) for k in range(kvl)])
        else:
            old_dots = dot_t(q_r, short_keys[r - 1])
        old_score = jnp.where(old_mask, old_dots * SCALE, HIDDEN_SCORE)
        new_score = jnp.where(new_mask, dot_t(q_r, k_r) * SCALE, HIDDEN_SCORE)
        top = jnp.maximum(
            jnp.max(old_score, axis=-1, keepdims=True), jnp.max(new_score, axis=-1, keepdims=True)
        )
        old_w = jnp.where(old_mask, jnp.exp(old_score - top), 0.0)
        new_w = jnp.where(new_mask, jnp.exp(new_score - top), 0.0)
        total = jnp.sum(old_w, axis=-1, keepdims=True) + jnp.sum(new_w, axis=-1, keepdims=True)
        old_w = old_w.astype(BF16)
        if r == 0:
            acc = by_kv([dot_t(old_w, lv_v[k]) for k in range(kvl)])
        else:
            acc = dot(old_w, short_values[r - 1])
        acc = acc + dot(new_w.astype(BF16), v_r)
        full = jnp.concatenate([acc, jnp.zeros((row_count, 128 - HD), F32)], axis=1)
        terms = []
        for number, count in ((top, 3), (total, 2)):
            rest = number
            for _ in range(count):
                term = rest.astype(BF16).astype(F32)
                terms.append(term)
                rest = rest - term
        for n, term in enumerate(terms):
            full = jnp.where(lane == HD + n, term, full)
        blocks.append(full)
    for t in range(steps):
        sb[t] = jnp.concatenate(
            [full[t * heads : (t + 1) * heads] for full in blocks], axis=0
        ).astype(BF16)

    s_copies = []
    for d in range(1, ns):
        target = lax.rem(me_s + d, ns)
        s_copies.append(
            to_seq(sb.at[target // copies_of_step], rb.at[d - 1], s_send, s_recv, d, target)
        )
    for copy in s_copies:
        copy.start()
    stream = [xg[c, my_step].astype(F32) for c in range(nt)]
    mate_stream = [xg[c, mate_step].astype(F32) for c in range(nt)]
    for copy in s_copies:
        copy.wait()
    parts = [sb[my_step]] + [rb[d] for d in range(ns - 1)]
    tops = [dot(part, spread_top) for part in parts]
    top = functools.reduce(jnp.maximum, tops)
    merged = jnp.zeros((m_rows, 128), F32)
    for part, part_top in zip(parts, tops):
        merged = merged + part.astype(F32) * jnp.exp(part_top - top)
    attended = merged[:, :HD] / (merged[:, HD + 3 : HD + 4] + merged[:, HD + 4 : HD + 5])
    attended = jnp.where(own_head, dot(attended.astype(BF16), spread_heads), 0.0).astype(BF16)
    attended = dot(join_heads, attended).astype(BF16)

    later[1].wait()
    head_parts, o_copies = [], []
    per = nt // 2
    for side in range(2):
        head_term = dot(attended, wo_v[:, side * per * dl : (side + 1) * per * dl])[:reqs]
        some = [head_term[:, c * dl : (c + 1) * dl] for c in range(per)]
        ob[side] = jnp.concatenate(some, axis=0).astype(BF16)
        head_parts += some
        for e in range(1, 2 * nt):
            copy = to_pair(
                ob.at[side], orb.at[side, e - 1], o_send.at[side], o_recv.at[side], e
            )
            copy.start()
            o_copies.append(copy)
    stream = [a + b for a, b in zip(stream, head_parts)]
    later[0].wait()
    gain = mg_v[...].astype(F32)[None]
    for copy in o_copies:
        copy.wait()

    def summed(slots):
        parts = []
        for side in range(2):
            got = orb[side, slots[0]].astype(F32)
            for slot in slots[1:]:
                got = got + orb[side, slot].astype(F32)
            parts += [got[c * reqs : (c + 1) * reqs] for c in range(per)]
        return parts

    stream = [a + b for a, b in zip(stream, summed(range(nt - 1)))]
    mate_stream = [a + b for a, b in zip(mate_stream, summed(range(nt - 1, 2 * nt - 1)))]
    both = [jnp.concatenate([a, b], axis=0) for a, b in zip(stream, mate_stream)]
    square = jnp.zeros((2 * reqs, 1), F32)
    for piece in both:
        square = square + jnp.sum(piece * piece, axis=-1, keepdims=True)
    inverse = lax.rsqrt(square * np.float32(1.0 / model) + EPS)
    mlp_in = [
        (piece * inverse * gain[:, c * dl : (c + 1) * dl]).astype(BF16)
        for c, piece in enumerate(both)
    ]
    later[2].wait()
    gate = project_t(mlp_in, wg_v)
    later[3].wait()
    lift = project_t(mlp_in, wu_v)
    hidden = gate / (1.0 + jnp.exp(-gate)) * lift
    if 2 * share > ff:
        shared = (iota((1, share), 1) < 2 * share - ff) & (half == 1)
        hidden = jnp.where(shared, 0.0, hidden)
    later[4].wait()
    down = dot(hidden.astype(BF16), wd_v[...])
    result = jnp.zeros((reqs, dl), F32)
    for c in range(nt):
        piece = down[:, c * dl : (c + 1) * dl]
        db[0, c] = piece[:reqs].astype(BF16)
        db[1, c] = piece[reqs:].astype(BF16)
        result = result + jnp.where(me_t == c, stream[c] + piece[:reqs], 0.0)
    d_copies = [
        to_pair(
            db.at[e // nt, lax.rem(me_t + e % nt, nt)], drb.at[e - 1], d_send, d_recv, e
        )
        for e in range(1, 2 * nt)
    ]
    for copy in d_copies:
        copy.start()
    for copy in d_copies:
        copy.wait()
    for e in range(2 * nt - 1):
        result = result + drb[e].astype(F32)
    fb[...] = result.astype(BF16)

    f_copies = []
    for d in range(1, steps):
        target = lax.rem(my_step + d, steps) * copies_of_step + my_twin
        f_copies.append(to_seq(fb, out.at[my_step], f_send, f_recv, d, target))
    for copy in f_copies:
        copy.start()
    own = pltpu.make_async_copy(fb, out.at[my_step], local_sem.at[14 + nt])
    own.start()
    for copy in f_copies:
        copy.wait()
    own.wait()


def body(
    ns, nt, tokens_in, attn_gain, mlp_gain, proj_query, proj_key, proj_value, proj_out,
    proj_gate, proj_up, proj_down, long_keys, long_values, short_keys, short_values,
    long_seen, short_len,
):
    steps, reqs, dl = tokens_in.shape
    ql = proj_query.shape[1]
    rows = steps * reqs
    m_rows = reqs * (ql // HD)
    index = (np.arange(ql) % HD) % HALF
    freq = (THETA ** (-2.0 * index.astype(np.float64) / HD)).astype(np.float32)[None]
    operands = (
        tokens_in, attn_gain, mlp_gain, proj_query, proj_key.T, proj_value.T,
        proj_out, proj_gate.T, proj_up.T, proj_down, long_keys.transpose(1, 2, 0),
        long_values.transpose(1, 2, 0), short_keys, short_values, jnp.asarray(freq),
    )
    ff = proj_down.shape[0]
    share = -(-ff // 32) * 16
    dma = pltpu.SemaphoreType.DMA
    return pl.pallas_call(
        functools.partial(kernel, ns, nt),
        out_shape=jax.ShapeDtypeStruct(tokens_in.shape, BF16),
        in_specs=[pl.BlockSpec(memory_space=pl.ANY)] * len(operands)
        + [pl.BlockSpec(memory_space=pltpu.SMEM)] * 2,
        out_specs=pl.BlockSpec(memory_space=pl.ANY),
        scratch_shapes=[
            pltpu.VMEM((share if a.shape[0] == ff else a.shape[0],) + a.shape[1:], a.dtype)
            for a in operands[1:]
        ]
        + [
            pltpu.VMEM((nt, steps, reqs, dl), BF16),
            pltpu.VMEM((steps, m_rows, 128), BF16),
            pltpu.VMEM((ns - 1, m_rows, 128), BF16),
            pltpu.VMEM((2, nt // 2 * reqs, dl), BF16),
            pltpu.VMEM((2, 2 * nt - 1, nt // 2 * reqs, dl), BF16),
            pltpu.VMEM((2, nt, reqs, dl), BF16),
            pltpu.VMEM((2 * nt - 1, reqs, dl), BF16),
            pltpu.VMEM((reqs, dl), BF16),
            dma((15 + nt,)),
            dma((nt - 1,)), dma((nt - 1,)),
            dma((ns - 1,)), dma((ns - 1,)),
            dma((2, 2 * nt - 1)), dma((2, 2 * nt - 1)),
            dma((2 * nt - 1,)), dma((2 * nt - 1,)),
            dma((steps - 1,)), dma((steps - 1,)),
        ],
        compiler_params=pltpu.CompilerParams(
            collective_id=0, has_side_effects=True, vmem_limit_bytes=60 * 1024 * 1024
        ),
    )(*operands, long_seen, short_len)


def solution(mesh):
    ns, nt = mesh.shape["seq"], mesh.shape["tp"]
    in_specs = (
        P(None, None, "tp"),
        P(),
        P(),
        P(None, "tp"),
        P(None, "tp"),
        P(None, "tp"),
        P("tp", None),
        P(None, "tp"),
        P(None, "tp"),
        P("tp", None),
        P("seq", "tp", None),
        P("seq", "tp", None),
        P("seq", "tp", None),
        P("seq", "tp", None),
        P(),
        P(),
    )
    return jax.shard_map(
        functools.partial(body, ns, nt),
        mesh=mesh,
        in_specs=in_specs,
        out_specs=P(None, None, "tp"),
        check_vma=False,
    )
```

```python
import functools
import math

import jax
import jax.numpy as jnp
import numpy as np
from jax import lax
from jax.experimental import pallas as pl
from jax.experimental.pallas import tpu as pltpu
from jax.sharding import PartitionSpec as P

HEADS = 32
KV_HEADS = 8
HD = 80
HALF = HD // 2
GROUP = HEADS // KV_HEADS
WIN = 4096
STEPS = 8

EPS = 1e-05
THETA = 10000.0
HIDDEN_SCORE = -1e30
SCALE = 1.0 / math.sqrt(HD)
F32 = jnp.float32
BF16 = jnp.bfloat16
MESH = pl.DeviceIdType.MESH


def dot(a, b):
    return lax.dot_general(a, b, (((1,), (0,)), ((), ())), preferred_element_type=F32)


def dot_t(a, b):
    return lax.dot_general(a, b, (((1,), (1,)), ((), ())), preferred_element_type=F32)


def pad_rows(v, rows):
    if v.shape[0] == rows:
        return v
    return jnp.concatenate([v, jnp.zeros((rows - v.shape[0], v.shape[1]), v.dtype)], axis=0)


def iota(shape, axis):
    return lax.broadcasted_iota(jnp.int32, shape, axis)


def flip(index, mask):
    bit = 1
    while bit <= mask:
        if mask & bit:
            index = index + bit - 2 * bit * (index // bit % 2)
        bit *= 2
    return index


def one_hot(condition):
    return jnp.where(condition, 1.0, 0.0).astype(BF16)


def sine_cosine(angle):
    turns = jnp.floor(angle * np.float32(2.0 / math.pi) + 0.5)
    rest = angle - turns * np.float32(1.5703125)
    rest = rest - turns * np.float32(4.8351287841796875e-4)
    rest = rest - turns * np.float32(math.pi / 2 - 1.5703125 - 4.8351287841796875e-4)
    sq = rest * rest
    sine = rest + rest * sq * (
        np.float32(-1.6666654611e-1)
        + sq * (np.float32(8.3321608736e-3) + sq * np.float32(-1.9515295891e-4))
    )
    cosine = 1.0 - 0.5 * sq + sq * sq * (
        np.float32(4.166664568298827e-2)
        + sq * (np.float32(-1.388731625493765e-3) + sq * np.float32(2.443315711809948e-5))
    )
    quarter = turns - 4.0 * jnp.floor(turns * 0.25)
    odd = (quarter == 1.0) | (quarter == 3.0)
    sin_out = jnp.where(odd, cosine, sine)
    cos_out = jnp.where(odd, sine, cosine)
    sin_out = jnp.where(quarter >= 2.0, -sin_out, sin_out)
    cos_out = jnp.where((quarter == 1.0) | (quarter == 2.0), -cos_out, cos_out)
    return sin_out, cos_out


def rope(v, cosine, signed_sine, front):
    ahead = jnp.concatenate([v[:, HALF:], v[:, :HALF]], axis=1)
    behind = jnp.concatenate([v[:, -HALF:], v[:, :-HALF]], axis=1)
    return v * cosine + jnp.where(front, ahead, behind) * signed_sine


def kernel(
    ns, nt, tok, ag, mg, wq, wk, wv, wo, wg, wu, wd, lk, lv, sk, sv, fr, seen, slen, out,
    ag_v, mg_v, wq_v, wk_v, wv_v, wo_v, wg_v, wu_v, wd_v, lk_v, lv_v, sk_v, sv_v, fr_v,
    xg, sb, rb, ob, orb, db, drb, fb, local_sem,
    x_send, x_recv, s_send, s_recv, o_send, o_recv, d_send, d_recv, f_send, f_recv,
):
    me_s = lax.axis_index("seq")
    me_t = lax.axis_index("tp")
    steps, reqs, dl = tok.shape
    rows = steps * reqs
    copies_of_step = ns // steps
    my_step = me_s // copies_of_step
    my_twin = lax.rem(me_s, copies_of_step)
    half = lax.rem(my_step, 2)
    mate_step = my_step + 1 - 2 * half
    mate = mate_step * copies_of_step + my_twin
    ff, share = wd.shape[0], wd_v.shape[0]
    low = pl.multiple_of(half * (ff - share), 16)
    model = wq.shape[0]
    ql = wq.shape[1]
    kl = wk.shape[0]
    heads = ql // HD
    kvl = kl // HD
    long_slots = lk.shape[2]
    short_slots = sk.shape[0]

    barrier = pltpu.get_barrier_semaphore()
    for d in range(1, nt):
        pl.semaphore_signal(
            barrier, inc=1, device_id=(me_s, lax.rem(me_t + d, nt)), device_id_type=MESH
        )
    for d in range(1, ns):
        pl.semaphore_signal(
            barrier, inc=1, device_id=(lax.rem(me_s + d, ns), me_t), device_id_type=MESH
        )

    for d in range(1, nt):
        pl.semaphore_signal(
            barrier, inc=1, device_id=(mate, lax.rem(me_t + d, nt)), device_id_type=MESH
        )

    def load(n, src, dst):
        return pltpu.make_async_copy(src, dst, local_sem.at[n])

    first = [
        load(0, wk, wk_v), load(1, wv, wv_v), load(2, fr, fr_v), load(3, ag, ag_v),
        load(4, tok, xg.at[me_t]),
    ]
    first += [
        load(5 + c, wq.at[pl.ds(c * dl, dl)], wq_v.at[pl.ds(c * dl, dl)]) for c in range(nt)
    ]
    cached = [
        load(5 + nt + n, src, dst)
        for n, (src, dst) in enumerate([(lk, lk_v), (sk, sk_v), (lv, lv_v), (sv, sv_v)])
    ]
    later = [
        load(9 + nt + n, src, dst)
        for n, (src, dst) in enumerate(
            [
                (mg, mg_v),
                (wo, wo_v),
                (wg.at[pl.ds(low, share)], wg_v),
                (wu.at[pl.ds(low, share)], wu_v),
                (wd.at[pl.ds(low, share)], wd_v),
            ]
        )
    ]
    for copy in first + cached:
        copy.start()

    def to_pair(src, dst, send, recv, e):
        return pltpu.make_async_remote_copy(
            src_ref=src, dst_ref=dst, send_sem=send.at[e - 1], recv_sem=recv.at[e - 1],
            device_id=(me_s if e < nt else mate, lax.rem(me_t + e % nt, nt)),
            device_id_type=MESH,
        )

    def to_seq(src, dst, send, recv, d, target):
        return pltpu.make_async_remote_copy(
            src_ref=src, dst_ref=dst, send_sem=send.at[d - 1], recv_sem=recv.at[d - 1],
            device_id=(target, me_t), device_id_type=MESH,
        )

    pl.semaphore_wait(barrier, nt - 1 + ns - 1 + nt - 1)
    x_copies = [
        pltpu.make_async_remote_copy(
            src_ref=tok, dst_ref=xg.at[me_t], send_sem=x_send.at[d - 1],
            recv_sem=x_recv.at[d - 1], device_id=(me_s, flip(me_t, d)), device_id_type=MESH,
        )
        for d in range(1, nt)
    ]
    for copy in x_copies:
        copy.start()

    first[2].wait()
    row = iota((rows, 1), 0)
    req = row % reqs
    base = jnp.where(req == 0, seen[0], 0)
    for r in range(1, reqs):
        base = jnp.where(req == r, slen[r - 1], base)
    position = (base + row // reqs).astype(F32)
    sine, cosine = sine_cosine(position * fr_v[...])
    front = iota((rows, ql), 1) % HD < HALF
    signed_sine = jnp.where(front, -sine, sine)
    q_rows, k_rows, m_rows = rows * heads, rows * kvl, reqs * heads
    i = iota((q_rows, 1), 0)
    order_q = one_hot(
        iota((q_rows, q_rows), 1)
        == (i % heads) * rows + (i // heads % steps) * reqs + i // (heads * steps)
    )
    i = iota((k_rows, 1), 0)
    order_k = one_hot(
        iota((k_rows, k_rows), 1)
        == (i // steps % kvl) * rows + (i % steps) * reqs + i // (steps * kvl)
    )
    lane128 = iota((128, 128), 0)
    spread_top = one_hot((lane128 >= HD) & (lane128 < HD + 3))
    spread_heads = one_hot(iota((HD, ql), 1) % HD == iota((HD, ql), 0))
    own_head = iota((m_rows, ql), 1) // HD == iota((m_rows, ql), 0) % heads
    join_heads = one_hot(iota((8, m_rows), 1) // heads == iota((8, m_rows), 0))

    for n, copy in enumerate(first + cached):
        if n != 2:
            copy.wait()
    for copy in later:
        copy.start()
    short_k = sk_v[...].reshape(short_slots * kvl, sk.shape[2])
    short_v = sv_v[...].reshape(short_slots * kvl, sv.shape[2])
    row_count = heads * steps
    new_count = kvl * steps
    i = iota((row_count, 1), 0)
    step_of = i // heads
    kv_of = i % heads // GROUP
    new_col = iota((1, new_count), 1)
    new_mask = (kv_of == new_col // steps) & (new_col % steps <= step_of) & (me_s == 0)
    lane = iota((row_count, 128), 1)

    def by_kv(terms):
        total = terms[0]
        for k in range(1, kvl):
            total = jnp.where(kv_of == k, terms[k], total)
        return total

    short_keys = [short_k[:, r * HD : (r + 1) * HD] for r in range(reqs - 1)]
    short_values = [short_v[:, r * HD : (r + 1) * HD] for r in range(reqs - 1)]
    slot = me_s * long_slots + iota((1, long_slots), 1)
    old_masks = [((slot - seen[0]) & (WIN - 1)) > step_of]
    col = iota((1, short_slots * kvl), 1)
    slot = me_s * short_slots + col // kvl
    same_kv = kv_of == col % kvl
    old_masks += [same_kv & (slot < slen[r]) for r in range(reqs - 1)]

    gain = ag_v[...].astype(F32)[None]
    gains = [gain[:, c * dl : (c + 1) * dl] for c in range(nt)]
    square = jnp.zeros((rows, 1), F32)
    query = jnp.zeros((rows, ql), F32)
    key = jnp.zeros((rows, kl), F32)
    value = jnp.zeros((rows, kl), F32)
    in_turn = dl % 128 == 0
    if not in_turn:
        for copy in x_copies:
            copy.wait()
    for d in range(nt):
        if in_turn:
            if d:
                x_copies[d - 1].wait()
            c = flip(me_t, d)
            here = pl.ds(pl.multiple_of(c * dl, 128), dl)
            gain = gains[0]
            for n in range(1, nt):
                gain = jnp.where(c == n, gains[n], gain)
        else:
            c, here, gain = d, pl.ds(d * dl, dl), gains[d]
        piece = xg[c].astype(F32).reshape(rows, dl)
        square = square + jnp.sum(piece * piece, axis=-1, keepdims=True)
        piece = (piece * gain).astype(BF16)
        key = key + dot_t(piece, wk_v[:, here])
        value = value + dot_t(piece, wv_v[:, here])
        query = query + dot(piece, wq_v[here, :])
    inverse = lax.rsqrt(square * np.float32(1.0 / model) + EPS)

    def units_by_rows(parts, weight):
        total = None
        for c, part in enumerate(parts):
            term = dot_t(weight[:, c * dl : (c + 1) * dl], part)
            total = term if total is None else total + term
        return total

    def stack(v, count):
        return jnp.concatenate([v[:, k * HD : (k + 1) * HD] for k in range(count)], axis=0)

    key = rope(key * inverse, cosine[:, :kl], signed_sine[:, :kl], front[:, :kl])
    value = value * inverse
    query = rope(query * inverse, cosine, signed_sine, front)
    key = dot(order_k, stack(key, kvl).astype(BF16))
    value = dot(order_k, stack(value, kvl).astype(BF16))
    query = dot(order_q, stack(query, heads).astype(BF16))

    blocks = []
    for r in range(reqs):
        q_r = query[r * row_count : (r + 1) * row_count].astype(BF16)
        k_r = key[r * new_count : (r + 1) * new_count].astype(BF16)
        v_r = value[r * new_count : (r + 1) * new_count].astype(BF16)
        old_mask = old_masks[r]
        if r == 0:
            old_dots = by_kv([dot(q_r, lk_v[k]) for k in range(kvl)])
        else:
            old_dots = dot_t(q_r, short_keys[r - 1])
        old_score = jnp.where(old_mask, old_dots * SCALE, HIDDEN_SCORE)
        new_score = jnp.where(new_mask, dot_t(q_r, k_r) * SCALE, HIDDEN_SCORE)
        top = jnp.maximum(
            jnp.max(old_score, axis=-1, keepdims=True), jnp.max(new_score, axis=-1, keepdims=True)
        )
        old_w = jnp.where(old_mask, jnp.exp(old_score - top), 0.0)
        new_w = jnp.where(new_mask, jnp.exp(new_score - top), 0.0)
        total = jnp.sum(old_w, axis=-1, keepdims=True) + jnp.sum(new_w, axis=-1, keepdims=True)
        old_w = old_w.astype(BF16)
        if r == 0:
            acc = by_kv([dot_t(old_w, lv_v[k]) for k in range(kvl)])
        else:
            acc = dot(old_w, short_values[r - 1])
        acc = acc + dot(new_w.astype(BF16), v_r)
        full = jnp.concatenate([acc, jnp.zeros((row_count, 128 - HD), F32)], axis=1)
        terms = []
        for number, count in ((top, 3), (total, 2)):
            rest = number
            for _ in range(count):
                term = rest.astype(BF16).astype(F32)
                terms.append(term)
                rest = rest - term
        for n, term in enumerate(terms):
            full = jnp.where(lane == HD + n, term, full)
        blocks.append(full)
    for t in range(steps):
        sb[t] = jnp.concatenate(
            [full[t * heads : (t + 1) * heads] for full in blocks], axis=0
        ).astype(BF16)

    s_copies = []
    for d in range(1, ns):
        target = lax.rem(me_s + d, ns)
        s_copies.append(
            to_seq(sb.at[target // copies_of_step], rb.at[d - 1], s_send, s_recv, d, target)
        )
    for copy in s_copies:
        copy.start()
    stream = [xg[c, my_step].astype(F32) for c in range(nt)]
    mate_stream = [xg[c, mate_step].astype(F32) for c in range(nt)]
    for copy in s_copies:
        copy.wait()
    parts = [sb[my_step]] + [rb[d] for d in range(ns - 1)]
    tops = [dot(part, spread_top) for part in parts]
    top = functools.reduce(jnp.maximum, tops)
    merged = jnp.zeros((m_rows, 128), F32)
    for part, part_top in zip(parts, tops):
        merged = merged + part.astype(F32) * jnp.exp(part_top - top)
    attended = merged[:, :HD] / (merged[:, HD + 3 : HD + 4] + merged[:, HD + 4 : HD + 5])
    attended = jnp.where(own_head, dot(attended.astype(BF16), spread_heads), 0.0).astype(BF16)
    attended = dot(join_heads, attended).astype(BF16)

    later[1].wait()
    head_parts, o_copies = [], []
    per = nt // 2
    for side in range(2):
        head_term = dot(attended, wo_v[:, side * per * dl : (side + 1) * per * dl])[:reqs]
        some = [head_term[:, c * dl : (c + 1) * dl] for c in range(per)]
        ob[side] = jnp.concatenate(some, axis=0).astype(BF16)
        head_parts += some
        for e in range(1, 2 * nt):
            copy = to_pair(
                ob.at[side], orb.at[side, e - 1], o_send.at[side], o_recv.at[side], e
            )
            copy.start()
            o_copies.append(copy)
    stream = [a + b for a, b in zip(stream, head_parts)]
    later[0].wait()
    gain = mg_v[...].astype(F32)[None]
    for copy in o_copies:
        copy.wait()

    def summed(slots):
        parts = []
        for side in range(2):
            got = orb[side, slots[0]].astype(F32)
            for slot in slots[1:]:
                got = got + orb[side, slot].astype(F32)
            parts += [got[c * reqs : (c + 1) * reqs] for c in range(per)]
        return parts

    stream = [a + b for a, b in zip(stream, summed(range(nt - 1)))]
    mate_stream = [a + b for a, b in zip(mate_stream, summed(range(nt - 1, 2 * nt - 1)))]
    both = [jnp.concatenate([a, b], axis=0) for a, b in zip(stream, mate_stream)]
    square = jnp.zeros((2 * reqs, 1), F32)
    for piece in both:
        square = square + jnp.sum(piece * piece, axis=-1, keepdims=True)
    inverse = lax.rsqrt(square * np.float32(1.0 / model) + EPS)
    mlp_in = [
        (piece * inverse * gain[:, c * dl : (c + 1) * dl]).astype(BF16)
        for c, piece in enumerate(both)
    ]
    later[2].wait()
    gate = units_by_rows(mlp_in, wg_v)
    later[3].wait()
    lift = units_by_rows(mlp_in, wu_v)
    hidden = gate / (1.0 + jnp.exp(-gate)) * lift
    if 2 * share > ff:
        shared = (iota((share, 1), 0) < 2 * share - ff) & (half == 1)
        hidden = jnp.where(shared, 0.0, hidden)
    identity = one_hot(iota((8, 8), 0) == iota((8, 8), 1))
    hidden = dot_t(identity, hidden.astype(BF16)).astype(BF16)
    later[4].wait()
    down = dot(hidden, wd_v[...])
    result = jnp.zeros((reqs, dl), F32)
    for c in range(nt):
        piece = down[:, c * dl : (c + 1) * dl]
        db[0, c] = piece[:reqs].astype(BF16)
        db[1, c] = piece[reqs:].astype(BF16)
        result = result + jnp.where(me_t == c, stream[c] + piece[:reqs], 0.0)
    d_copies = [
        to_pair(
            db.at[e // nt, lax.rem(me_t + e % nt, nt)], drb.at[e - 1], d_send, d_recv, e
        )
        for e in range(1, 2 * nt)
    ]
    for copy in d_copies:
        copy.start()
    for copy in d_copies:
        copy.wait()
    for e in range(2 * nt - 1):
        result = result + drb[e].astype(F32)
    fb[...] = result.astype(BF16)

    f_copies = []
    for d in range(1, steps):
        target = lax.rem(my_step + d, steps) * copies_of_step + my_twin
        f_copies.append(to_seq(fb, out.at[my_step], f_send, f_recv, d, target))
    for copy in f_copies:
        copy.start()
    own = pltpu.make_async_copy(fb, out.at[my_step], local_sem.at[14 + nt])
    own.start()
    for copy in f_copies:
        copy.wait()
    own.wait()


def body(
    ns, nt, tokens_in, attn_gain, mlp_gain, proj_query, proj_key, proj_value, proj_out,
    proj_gate, proj_up, proj_down, long_keys, long_values, short_keys, short_values,
    long_seen, short_len,
):
    steps, reqs, dl = tokens_in.shape
    ql = proj_query.shape[1]
    rows = steps * reqs
    m_rows = reqs * (ql // HD)
    index = (np.arange(ql) % HD) % HALF
    freq = (THETA ** (-2.0 * index.astype(np.float64) / HD)).astype(np.float32)[None]
    operands = (
        tokens_in, attn_gain, mlp_gain, proj_query, proj_key.T, proj_value.T,
        proj_out, proj_gate.T, proj_up.T, proj_down, long_keys.transpose(1, 2, 0),
        long_values.transpose(1, 2, 0), short_keys, short_values, jnp.asarray(freq),
    )
    ff = proj_down.shape[0]
    share = -(-ff // 32) * 16
    dma = pltpu.SemaphoreType.DMA
    return pl.pallas_call(
        functools.partial(kernel, ns, nt),
        out_shape=jax.ShapeDtypeStruct(tokens_in.shape, BF16),
        in_specs=[pl.BlockSpec(memory_space=pl.ANY)] * len(operands)
        + [pl.BlockSpec(memory_space=pltpu.SMEM)] * 2,
        out_specs=pl.BlockSpec(memory_space=pl.ANY),
        scratch_shapes=[
            pltpu.VMEM((share if a.shape[0] == ff else a.shape[0],) + a.shape[1:], a.dtype)
            for a in operands[1:]
        ]
        + [
            pltpu.VMEM((nt, steps, reqs, dl), BF16),
            pltpu.VMEM((steps, m_rows, 128), BF16),
            pltpu.VMEM((ns - 1, m_rows, 128), BF16),
            pltpu.VMEM((2, nt // 2 * reqs, dl), BF16),
            pltpu.VMEM((2, 2 * nt - 1, nt // 2 * reqs, dl), BF16),
            pltpu.VMEM((2, nt, reqs, dl), BF16),
            pltpu.VMEM((2 * nt - 1, reqs, dl), BF16),
            pltpu.VMEM((reqs, dl), BF16),
            dma((15 + nt,)),
            dma((nt - 1,)), dma((nt - 1,)),
            dma((ns - 1,)), dma((ns - 1,)),
            dma((2, 2 * nt - 1)), dma((2, 2 * nt - 1)),
            dma((2 * nt - 1,)), dma((2 * nt - 1,)),
            dma((steps - 1,)), dma((steps - 1,)),
        ],
        compiler_params=pltpu.CompilerParams(
            collective_id=0, has_side_effects=True, vmem_limit_bytes=60 * 1024 * 1024
        ),
    )(*operands, long_seen, short_len)


def solution(mesh):
    ns, nt = mesh.shape["seq"], mesh.shape["tp"]
    in_specs = (
        P(None, None, "tp"),
        P(),
        P(),
        P(None, "tp"),
        P(None, "tp"),
        P(None, "tp"),
        P("tp", None),
        P(None, "tp"),
        P(None, "tp"),
        P("tp", None),
        P("seq", "tp", None),
        P("seq", "tp", None),
        P("seq", "tp", None),
        P("seq", "tp", None),
        P(),
        P(),
    )
    return jax.shard_map(
        functools.partial(body, ns, nt),
        mesh=mesh,
        in_specs=in_specs,
        out_specs=P(None, None, "tp"),
        check_vma=False,
    )
```

```python
import functools
import math

import jax
import jax.numpy as jnp
import numpy as np
from jax import lax
from jax.experimental import pallas as pl
from jax.experimental.pallas import tpu as pltpu
from jax.sharding import PartitionSpec as P

HEADS = 32
KV_HEADS = 8
HD = 80
HALF = HD // 2
GROUP = HEADS // KV_HEADS
WIN = 4096
STEPS = 8

EPS = 1e-05
THETA = 10000.0
HIDDEN_SCORE = -1e30
SCALE = 1.0 / math.sqrt(HD)
F32 = jnp.float32
BF16 = jnp.bfloat16
MESH = pl.DeviceIdType.MESH


def dot(a, b):
    return lax.dot_general(a, b, (((1,), (0,)), ((), ())), preferred_element_type=F32)


def dot_t(a, b):
    return lax.dot_general(a, b, (((1,), (1,)), ((), ())), preferred_element_type=F32)


def pad_rows(v, rows):
    if v.shape[0] == rows:
        return v
    return jnp.concatenate([v, jnp.zeros((rows - v.shape[0], v.shape[1]), v.dtype)], axis=0)


def iota(shape, axis):
    return lax.broadcasted_iota(jnp.int32, shape, axis)


def flip(index, mask):
    bit = 1
    while bit <= mask:
        if mask & bit:
            index = index + bit - 2 * bit * (index // bit % 2)
        bit *= 2
    return index


def far_first(copies):
    order = sorted(range(len(copies)), key=lambda n: abs(2 * n + 1 - len(copies)))
    return [copies[n] for n in order]


def one_hot(condition):
    return jnp.where(condition, 1.0, 0.0).astype(BF16)


def sine_cosine(angle):
    turns = jnp.floor(angle * np.float32(2.0 / math.pi) + 0.5)
    rest = angle - turns * np.float32(1.5703125)
    rest = rest - turns * np.float32(4.8351287841796875e-4)
    rest = rest - turns * np.float32(math.pi / 2 - 1.5703125 - 4.8351287841796875e-4)
    sq = rest * rest
    sine = rest + rest * sq * (
        np.float32(-1.6666654611e-1)
        + sq * (np.float32(8.3321608736e-3) + sq * np.float32(-1.9515295891e-4))
    )
    cosine = 1.0 - 0.5 * sq + sq * sq * (
        np.float32(4.166664568298827e-2)
        + sq * (np.float32(-1.388731625493765e-3) + sq * np.float32(2.443315711809948e-5))
    )
    quarter = turns - 4.0 * jnp.floor(turns * 0.25)
    odd = (quarter == 1.0) | (quarter == 3.0)
    sin_out = jnp.where(odd, cosine, sine)
    cos_out = jnp.where(odd, sine, cosine)
    sin_out = jnp.where(quarter >= 2.0, -sin_out, sin_out)
    cos_out = jnp.where((quarter == 1.0) | (quarter == 2.0), -cos_out, cos_out)
    return sin_out, cos_out


def rope(v, cosine, signed_sine, front):
    ahead = jnp.concatenate([v[:, HALF:], v[:, :HALF]], axis=1)
    behind = jnp.concatenate([v[:, -HALF:], v[:, :-HALF]], axis=1)
    return v * cosine + jnp.where(front, ahead, behind) * signed_sine


def kernel(
    ns, nt, tok, ag, mg, wq, wk, wv, wo, wg, wu, wd, lk, lv, sk, sv, fr, seen, slen, out,
    ag_v, mg_v, wq_v, wk_v, wv_v, wo_v, wg_v, wu_v, wd_v, lk_v, lv_v, sk_v, sv_v, fr_v,
    xg, sb, rb, ob, orb, db, drb, fb, local_sem,
    x_send, x_recv, s_send, s_recv, o_send, o_recv, d_send, d_recv, f_send, f_recv,
):
    me_s = lax.axis_index("seq")
    me_t = lax.axis_index("tp")
    steps, reqs, dl = tok.shape
    rows = steps * reqs
    copies_of_step = ns // steps
    my_step = me_s // copies_of_step
    my_twin = lax.rem(me_s, copies_of_step)
    half = lax.rem(my_step, 2)
    mate_step = my_step + 1 - 2 * half
    mate = mate_step * copies_of_step + my_twin
    ff, share = wd.shape[0], wd_v.shape[0]
    low = pl.multiple_of(half * (ff - share), 16)
    model = wq.shape[0]
    ql = wq.shape[1]
    kl = wk.shape[0]
    heads = ql // HD
    kvl = kl // HD
    long_slots = lk.shape[2]
    short_slots = sk.shape[0]

    barrier = pltpu.get_barrier_semaphore()
    for d in range(1, nt):
        pl.semaphore_signal(
            barrier, inc=1, device_id=(me_s, lax.rem(me_t + d, nt)), device_id_type=MESH
        )
    for d in range(1, ns):
        pl.semaphore_signal(
            barrier, inc=1, device_id=(lax.rem(me_s + d, ns), me_t), device_id_type=MESH
        )

    for d in range(1, nt):
        pl.semaphore_signal(
            barrier, inc=1, device_id=(mate, lax.rem(me_t + d, nt)), device_id_type=MESH
        )

    def load(n, src, dst):
        return pltpu.make_async_copy(src, dst, local_sem.at[n])

    first = [
        load(0, wk, wk_v), load(1, wv, wv_v), load(2, fr, fr_v), load(3, ag, ag_v),
        load(4, tok, xg.at[me_t]),
    ]
    first += [
        load(5 + c, wq.at[pl.ds(c * dl, dl)], wq_v.at[pl.ds(c * dl, dl)]) for c in range(nt)
    ]
    cached = [
        load(5 + nt + n, src, dst)
        for n, (src, dst) in enumerate([(lk, lk_v), (sk, sk_v), (lv, lv_v), (sv, sv_v)])
    ]
    later = [
        load(9 + nt + n, src, dst)
        for n, (src, dst) in enumerate(
            [
                (mg, mg_v),
                (wo, wo_v),
                (wg.at[pl.ds(low, share)], wg_v),
                (wu.at[pl.ds(low, share)], wu_v),
                (wd.at[pl.ds(low, share)], wd_v),
            ]
        )
    ]
    for copy in first + cached:
        copy.start()

    def to_pair(src, dst, send, recv, e):
        return pltpu.make_async_remote_copy(
            src_ref=src, dst_ref=dst, send_sem=send.at[e - 1], recv_sem=recv.at[e - 1],
            device_id=(me_s if e < nt else mate, lax.rem(me_t + e % nt, nt)),
            device_id_type=MESH,
        )

    def to_seq(src, dst, send, recv, d, target):
        return pltpu.make_async_remote_copy(
            src_ref=src, dst_ref=dst, send_sem=send.at[d - 1], recv_sem=recv.at[d - 1],
            device_id=(target, me_t), device_id_type=MESH,
        )

    pl.semaphore_wait(barrier, nt - 1 + ns - 1 + nt - 1)
    x_copies = [
        pltpu.make_async_remote_copy(
            src_ref=tok, dst_ref=xg.at[me_t], send_sem=x_send.at[d - 1],
            recv_sem=x_recv.at[d - 1], device_id=(me_s, flip(me_t, d)), device_id_type=MESH,
        )
        for d in range(1, nt)
    ]
    for copy in x_copies:
        copy.start()

    first[2].wait()
    row = iota((rows, 1), 0)
    req = row % reqs
    base = jnp.where(req == 0, seen[0], 0)
    for r in range(1, reqs):
        base = jnp.where(req == r, slen[r - 1], base)
    position = (base + row // reqs).astype(F32)
    sine, cosine = sine_cosine(position * fr_v[...])
    front = iota((rows, ql), 1) % HD < HALF
    signed_sine = jnp.where(front, -sine, sine)
    q_rows, k_rows, m_rows = rows * heads, rows * kvl, reqs * heads
    i = iota((q_rows, 1), 0)
    order_q = one_hot(
        iota((q_rows, q_rows), 1)
        == (i % heads) * rows + (i // heads % steps) * reqs + i // (heads * steps)
    )
    i = iota((k_rows, 1), 0)
    order_k = one_hot(
        iota((k_rows, k_rows), 1)
        == (i // steps % kvl) * rows + (i % steps) * reqs + i // (steps * kvl)
    )
    lane128 = iota((128, 128), 0)
    spread_top = one_hot((lane128 >= HD) & (lane128 < HD + 3))
    spread_heads = one_hot(iota((HD, ql), 1) % HD == iota((HD, ql), 0))
    own_head = iota((m_rows, ql), 1) // HD == iota((m_rows, ql), 0) % heads
    join_heads = one_hot(iota((8, m_rows), 1) // heads == iota((8, m_rows), 0))

    for n, copy in enumerate(first + cached):
        if n != 2:
            copy.wait()
    for copy in later:
        copy.start()
    gain = ag_v[...].astype(F32)[None]
    gains = [gain[:, c * dl : (c + 1) * dl] for c in range(nt)]
    square = jnp.zeros((rows, 1), F32)
    query = jnp.zeros((rows, ql), F32)
    key = jnp.zeros((rows, kl), F32)
    value = jnp.zeros((rows, kl), F32)
    in_turn = dl % 128 == 0
    if not in_turn:
        for copy in x_copies:
            copy.wait()
    for d in range(nt):
        if in_turn:
            if d:
                x_copies[d - 1].wait()
            c = flip(me_t, d)
            here = pl.ds(pl.multiple_of(c * dl, 128), dl)
            gain = gains[0]
            for n in range(1, nt):
                gain = jnp.where(c == n, gains[n], gain)
        else:
            c, here, gain = d, pl.ds(d * dl, dl), gains[d]
        piece = xg[c].astype(F32).reshape(rows, dl)
        square = square + jnp.sum(piece * piece, axis=-1, keepdims=True)
        piece = (piece * gain).astype(BF16)
        key = key + dot_t(piece, wk_v[:, here])
        value = value + dot_t(piece, wv_v[:, here])
        query = query + dot(piece, wq_v[here, :])
    inverse = lax.rsqrt(square * np.float32(1.0 / model) + EPS)

    def project_t(parts, weight):
        total = None
        for c, part in enumerate(parts):
            term = dot_t(part, weight[:, c * dl : (c + 1) * dl])
            total = term if total is None else total + term
        return total

    def stack(v, count):
        return jnp.concatenate([v[:, k * HD : (k + 1) * HD] for k in range(count)], axis=0)

    key = rope(key * inverse, cosine[:, :kl], signed_sine[:, :kl], front[:, :kl])
    value = value * inverse
    query = rope(query * inverse, cosine, signed_sine, front)
    key = dot(order_k, stack(key, kvl).astype(BF16))
    value = dot(order_k, stack(value, kvl).astype(BF16))
    query = dot(order_q, stack(query, heads).astype(BF16))

    short_k = sk_v[...].reshape(short_slots * kvl, sk.shape[2])
    short_v = sv_v[...].reshape(short_slots * kvl, sv.shape[2])
    row_count = heads * steps
    new_count = kvl * steps
    i = iota((row_count, 1), 0)
    step_of = i // heads
    kv_of = i % heads // GROUP
    new_col = iota((1, new_count), 1)
    new_mask = (kv_of == new_col // steps) & (new_col % steps <= step_of) & (me_s == 0)
    lane = iota((row_count, 128), 1)

    def by_kv(terms):
        total = terms[0]
        for k in range(1, kvl):
            total = jnp.where(kv_of == k, terms[k], total)
        return total

    blocks = []
    for r in range(reqs):
        q_r = query[r * row_count : (r + 1) * row_count].astype(BF16)
        k_r = key[r * new_count : (r + 1) * new_count].astype(BF16)
        v_r = value[r * new_count : (r + 1) * new_count].astype(BF16)
        if r == 0:
            slot = me_s * long_slots + iota((1, long_slots), 1)
            old_mask = ((slot - seen[0]) & (WIN - 1)) > step_of
            old_dots = by_kv([dot(q_r, lk_v[k]) for k in range(kvl)])
        else:
            cut = slice((r - 1) * HD, r * HD)
            col = iota((1, short_slots * kvl), 1)
            slot = me_s * short_slots + col // kvl
            old_mask = (kv_of == col % kvl) & (slot < slen[r - 1])
            old_dots = dot_t(q_r, short_k[:, cut])
        old_score = jnp.where(old_mask, old_dots * SCALE, HIDDEN_SCORE)
        new_score = jnp.where(new_mask, dot_t(q_r, k_r) * SCALE, HIDDEN_SCORE)
        top = jnp.maximum(
            jnp.max(old_score, axis=-1, keepdims=True), jnp.max(new_score, axis=-1, keepdims=True)
        )
        old_w = jnp.where(old_mask, jnp.exp(old_score - top), 0.0)
        new_w = jnp.where(new_mask, jnp.exp(new_score - top), 0.0)
        total = jnp.sum(old_w, axis=-1, keepdims=True) + jnp.sum(new_w, axis=-1, keepdims=True)
        old_w = old_w.astype(BF16)
        if r == 0:
            acc = by_kv([dot_t(old_w, lv_v[k]) for k in range(kvl)])
        else:
            acc = dot(old_w, short_v[:, cut])
        acc = acc + dot(new_w.astype(BF16), v_r)
        full = jnp.concatenate([acc, jnp.zeros((row_count, 128 - HD), F32)], axis=1)
        terms = []
        for number, count in ((top, 3), (total, 2)):
            rest = number
            for _ in range(count):
                term = rest.astype(BF16).astype(F32)
                terms.append(term)
                rest = rest - term
        for n, term in enumerate(terms):
            full = jnp.where(lane == HD + n, term, full)
        blocks.append(full)
    for t in range(steps):
        sb[t] = jnp.concatenate(
            [full[t * heads : (t + 1) * heads] for full in blocks], axis=0
        ).astype(BF16)

    s_copies = []
    for d in range(1, ns):
        target = lax.rem(me_s + d, ns)
        s_copies.append(
            to_seq(sb.at[target // copies_of_step], rb.at[d - 1], s_send, s_recv, d, target)
        )
    for copy in far_first(s_copies):
        copy.start()
    stream = [xg[c, my_step].astype(F32) for c in range(nt)]
    mate_stream = [xg[c, mate_step].astype(F32) for c in range(nt)]
    for copy in s_copies:
        copy.wait()
    parts = [sb[my_step]] + [rb[d] for d in range(ns - 1)]
    tops = [dot(part, spread_top) for part in parts]
    top = functools.reduce(jnp.maximum, tops)
    merged = jnp.zeros((m_rows, 128), F32)
    for part, part_top in zip(parts, tops):
        merged = merged + part.astype(F32) * jnp.exp(part_top - top)
    attended = merged[:, :HD] / (merged[:, HD + 3 : HD + 4] + merged[:, HD + 4 : HD + 5])
    attended = jnp.where(own_head, dot(attended.astype(BF16), spread_heads), 0.0).astype(BF16)
    attended = dot(join_heads, attended).astype(BF16)

    later[1].wait()
    head_term = dot(attended, wo_v[...])[:reqs]
    head_parts = [head_term[:, c * dl : (c + 1) * dl] for c in range(nt)]
    ob[...] = jnp.concatenate(head_parts, axis=0).astype(BF16)
    o_copies = [to_pair(ob, orb.at[e - 1], o_send, o_recv, e) for e in range(1, 2 * nt)]
    for copy in o_copies:
        copy.start()
    stream = [a + b for a, b in zip(stream, head_parts)]
    later[0].wait()
    gain = mg_v[...].astype(F32)[None]
    for copy in o_copies:
        copy.wait()

    def summed(slots):
        got = orb[slots[0]].astype(F32)
        for slot in slots[1:]:
            got = got + orb[slot].astype(F32)
        return [got[c * reqs : (c + 1) * reqs] for c in range(nt)]

    stream = [a + b for a, b in zip(stream, summed(range(nt - 1)))]
    mate_stream = [a + b for a, b in zip(mate_stream, summed(range(nt - 1, 2 * nt - 1)))]
    both = [jnp.concatenate([a, b], axis=0) for a, b in zip(stream, mate_stream)]
    square = jnp.zeros((2 * reqs, 1), F32)
    for piece in both:
        square = square + jnp.sum(piece * piece, axis=-1, keepdims=True)
    inverse = lax.rsqrt(square * np.float32(1.0 / model) + EPS)
    mlp_in = [
        (piece * inverse * gain[:, c * dl : (c + 1) * dl]).astype(BF16)
        for c, piece in enumerate(both)
    ]
    later[2].wait()
    gate = project_t(mlp_in, wg_v)
    later[3].wait()
    lift = project_t(mlp_in, wu_v)
    hidden = gate / (1.0 + jnp.exp(-gate)) * lift
    if 2 * share > ff:
        shared = (iota((1, share), 1) < 2 * share - ff) & (half == 1)
        hidden = jnp.where(shared, 0.0, hidden)
    later[4].wait()
    down = dot(hidden.astype(BF16), wd_v[...])
    result = jnp.zeros((reqs, dl), F32)
    for c in range(nt):
        piece = down[:, c * dl : (c + 1) * dl]
        db[0, c] = piece[:reqs].astype(BF16)
        db[1, c] = piece[reqs:].astype(BF16)
        result = result + jnp.where(me_t == c, stream[c] + piece[:reqs], 0.0)
    d_copies = [
        to_pair(
            db.at[e // nt, lax.rem(me_t + e % nt, nt)], drb.at[e - 1], d_send, d_recv, e
        )
        for e in range(1, 2 * nt)
    ]
    for copy in d_copies:
        copy.start()
    for copy in d_copies:
        copy.wait()
    for e in range(2 * nt - 1):
        result = result + drb[e].astype(F32)
    fb[...] = result.astype(BF16)

    f_copies = []
    for d in range(1, steps):
        target = lax.rem(my_step + d, steps) * copies_of_step + my_twin
        f_copies.append(to_seq(fb, out.at[my_step], f_send, f_recv, d, target))
    for copy in far_first(f_copies):
        copy.start()
    own = pltpu.make_async_copy(fb, out.at[my_step], local_sem.at[14 + nt])
    own.start()
    for copy in f_copies:
        copy.wait()
    own.wait()


def body(
    ns, nt, tokens_in, attn_gain, mlp_gain, proj_query, proj_key, proj_value, proj_out,
    proj_gate, proj_up, proj_down, long_keys, long_values, short_keys, short_values,
    long_seen, short_len,
):
    steps, reqs, dl = tokens_in.shape
    ql = proj_query.shape[1]
    rows = steps * reqs
    m_rows = reqs * (ql // HD)
    index = (np.arange(ql) % HD) % HALF
    freq = (THETA ** (-2.0 * index.astype(np.float64) / HD)).astype(np.float32)[None]
    operands = (
        tokens_in, attn_gain, mlp_gain, proj_query, proj_key.T, proj_value.T,
        proj_out, proj_gate.T, proj_up.T, proj_down, long_keys.transpose(1, 2, 0),
        long_values.transpose(1, 2, 0), short_keys, short_values, jnp.asarray(freq),
    )
    ff = proj_down.shape[0]
    share = -(-ff // 32) * 16
    dma = pltpu.SemaphoreType.DMA
    return pl.pallas_call(
        functools.partial(kernel, ns, nt),
        out_shape=jax.ShapeDtypeStruct(tokens_in.shape, BF16),
        in_specs=[pl.BlockSpec(memory_space=pl.ANY)] * len(operands)
        + [pl.BlockSpec(memory_space=pltpu.SMEM)] * 2,
        out_specs=pl.BlockSpec(memory_space=pl.ANY),
        scratch_shapes=[
            pltpu.VMEM((share if a.shape[0] == ff else a.shape[0],) + a.shape[1:], a.dtype)
            for a in operands[1:]
        ]
        + [
            pltpu.VMEM((nt, steps, reqs, dl), BF16),
            pltpu.VMEM((steps, m_rows, 128), BF16),
            pltpu.VMEM((ns - 1, m_rows, 128), BF16),
            pltpu.VMEM((nt * reqs, dl), BF16),
            pltpu.VMEM((2 * nt - 1, nt * reqs, dl), BF16),
            pltpu.VMEM((2, nt, reqs, dl), BF16),
            pltpu.VMEM((2 * nt - 1, reqs, dl), BF16),
            pltpu.VMEM((reqs, dl), BF16),
            dma((15 + nt,)),
            dma((nt - 1,)), dma((nt - 1,)),
            dma((ns - 1,)), dma((ns - 1,)),
            dma((2 * nt - 1,)), dma((2 * nt - 1,)),
            dma((2 * nt - 1,)), dma((2 * nt - 1,)),
            dma((steps - 1,)), dma((steps - 1,)),
        ],
        compiler_params=pltpu.CompilerParams(
            collective_id=0, has_side_effects=True, vmem_limit_bytes=60 * 1024 * 1024
        ),
    )(*operands, long_seen, short_len)


def solution(mesh):
    ns, nt = mesh.shape["seq"], mesh.shape["tp"]
    in_specs = (
        P(None, None, "tp"),
        P(),
        P(),
        P(None, "tp"),
        P(None, "tp"),
        P(None, "tp"),
        P("tp", None),
        P(None, "tp"),
        P(None, "tp"),
        P("tp", None),
        P("seq", "tp", None),
        P("seq", "tp", None),
        P("seq", "tp", None),
        P("seq", "tp", None),
        P(),
        P(),
    )
    return jax.shard_map(
        functools.partial(body, ns, nt),
        mesh=mesh,
        in_specs=in_specs,
        out_specs=P(None, None, "tp"),
        check_vma=False,
    )
```
